512 devices in a mesh: samp: 64 (over y, z), feat: 8 (over x, core).
Axes of the slice: x: 4, y: 4, z: 16, core: 2. Of those that a mesh axis runs over, the one named last changes fastest.
Arguments:
- images: bfloat16 [32768, 3072], P('samp'), may hold values from -6 to 6, as said below
- labels: int32 [32768], P('samp'), may hold values from 0 to 999
- filters: bfloat16 [3, 128, 108], P(None, 'feat'), may hold values from -0.625 to 0.625
- biases: float32 [3, 128], P(None, 'feat'), may hold values from -3 to 3
Outputs:
- coefficients: float32 [1536, 1000], P(None, 'feat')
- residual: float32 [32768, 1000], P('samp', 'feat')
The draws below stay inside these ranges and needn't reach their ends.
Inputs may be any that keep to these rules, and one draw needn't show every extreme that they name: Every pixel intensity of the images lies between -6 and 6.
All inputs are finite; a program needn't handle non-finite values.
Results may differ from the reference program's by a relative error of at most 0.007.
The reference program's roundings to bfloat16 on the way (of `features`) count: a program that leaves them out, or rounds other values in their place, can miss the bound.
Values may be sent and summed in bfloat16 or wider, within the bound.
No kernel may reach another device: no remote copies, remote signals or barrier semaphores. Data moves between devices by JAX's collectives and lax.ppermute only.
A program may use at most 128 MiB of HBM per device.

```python
import math
import jax
import jax.numpy as jnp
from jax import lax

ROWS = 512
FILTERS = 128
CLS = 1000
BLOCKS = 3
IMG = 32
BLK = 512
SAMPLES = 32768
N_SAMP = 64


def smooth_pattern(base_key, image_count, exponent, harmonics):
    pixel_axis = jnp.arange(IMG, dtype=jnp.float32)
    vertical = pixel_axis[:, None]
    horizontal = pixel_axis[None, :]
    pattern = jnp.zeros((image_count, 3, IMG, IMG), jnp.float32)
    for harmonic in range(1, harmonics + 1):
        term_key = jax.random.fold_in(base_key, harmonic)
        freq_key, phase_key, shared_key, colour_key = jax.random.split(term_key, 4)
        frequency = jax.random.uniform(freq_key, (image_count, 2), jnp.float32, -1.0, 1.0) * (harmonic / (2.0 * IMG))
        phases = jax.random.uniform(phase_key, (image_count, 3), jnp.float32, -math.pi, math.pi)
        shared = jax.random.normal(shared_key, (image_count, 1), jnp.float32)
        colour = jax.random.normal(colour_key, (image_count, 3), jnp.float32)
        amplitude = (shared + 0.5 * colour) * float(harmonic) ** (-exponent)
        angles = 2.0 * math.pi * (frequency[:, 0, None, None, None] * vertical[None, None, :, :] + frequency[:, 1, None, None, None] * horizontal[None, None, :, :]) + phases[:, :, None, None]
        pattern = pattern + amplitude[:, :, None, None] * jnp.cos(angles)
    return pattern.reshape(image_count, 3 * IMG * IMG)


def draw_images(key, part):
    key = jax.random.fold_in(key, 11)
    pattern_key, noise_key, contrast_key = jax.random.split(key, 3)
    pattern = smooth_pattern(pattern_key, SAMPLES, 1.0, 24)
    noise = 0.3 * jax.random.normal(noise_key, (SAMPLES, 3 * IMG * IMG), jnp.float32)
    contrast = jnp.exp(jax.random.uniform(contrast_key, (SAMPLES, 1), jnp.float32, math.log(0.5), math.log(2.0)))
    values = contrast * (pattern + noise)
    return jnp.clip(values, -6.0, 6.0).astype(jnp.bfloat16)


def place_ends(entries, rng, least, largest):
    longest = entries.shape.index(max(entries.shape))
    spots = []
    for shift in (0, 1):
        where = [jax.random.randint(jax.random.fold_in(rng, axis), (), 0, length) for axis, length in enumerate(entries.shape)]
        where[longest] = (where[longest] + shift) % entries.shape[longest]
        spots.append(tuple(where))
    return entries.at[spots[0]].set(least).at[spots[1]].set(largest)


def steps_of(key, dims, shards, least, top_value):
    gain = 1.0
    for position, shards_of in shards:
        draws = jax.random.uniform(jax.random.fold_in(jax.random.fold_in(key, 6), position), (shards_of,), jnp.float32, least / len(shards), top_value / len(shards))
        gain = gain * jnp.repeat(jnp.exp(draws), dims[position] // shards_of).reshape((-1,) + (1,) * (len(dims) - 1 - position))
    return gain


def normal_values(own_key, extent, width, reach, cuts=(), held_as=jnp.bfloat16):
    values = jax.random.normal(own_key, extent, jnp.float32) * width
    if len(cuts) > 0:
        values = steps_of(own_key, extent, cuts, -0.22, 0.18) * values
    return jnp.clip(values, min=-reach, max=reach).astype(held_as)


def setup_inputs(seed: int = 0) -> dict:
    splits = jax.random.split(jax.random.key(seed), 5)
    return {
        "images": draw_images(jax.random.fold_in(splits[4], 71), 0),
        "labels": place_ends(jax.random.randint(splits[1], (SAMPLES,), 0, CLS), jax.random.fold_in(splits[1], 1), 0, CLS - 1).astype(jnp.int32),
        "filters": normal_values(splits[2], (BLOCKS, FILTERS, 108), 108 ** -0.5, 0.625, ((1, 8),)),
        "biases": normal_values(splits[3], (BLOCKS, FILTERS), 0.5, 3.0, ((1, 8),), jnp.float32),
    }


def featurize(pixels, kernels, offsets):
    row_count = pixels.shape[0]
    filter_count = kernels.shape[0]
    pictures = pixels.reshape(row_count, 3, 32, 32)
    weights = kernels.reshape(filter_count, 3, 6, 6)
    response = lax.conv_general_dilated(pictures, weights, (2, 2), 'VALID', dimension_numbers=('NCHW', 'OIHW', 'NCHW'), preferred_element_type=jnp.float32)
    rectified = jnp.maximum(response + offsets[None, :, None, None], 0.0)
    pooled = rectified.reshape(row_count, filter_count, 2, 7, 2, 7).mean(axis=(3, 5))
    return pooled.reshape(row_count, filter_count * 4).astype(jnp.bfloat16)

def reference(images, labels, filters, biases):
    total = images.shape[0]
    classes = jnp.arange(CLS, dtype=jnp.int32)
    residual = (labels[:, None] == classes[None, :]).astype(jnp.float32)
    pieces = images.reshape(N_SAMP, ROWS, images.shape[1])
    results = []
    for block_index in range(BLOCKS):
        kernels = filters[block_index]
        offsets = biases[block_index]
        made = lax.map(lambda piece: featurize(piece, kernels, offsets), pieces)
        features = made.reshape(total, BLK)
        gram = lax.dot_general(features.astype(jnp.float32), features.astype(jnp.float32), (((0,), (0,)), ((), ())), preferred_element_type=jnp.float32) / total
        ridge = 0.1 * jnp.trace(gram) / BLK + 1e-05
        wide = features.astype(jnp.float32)
        gradient = lax.dot_general(wide.astype(jnp.float32), residual.astype(jnp.float32), (((0,), (0,)), ((), ())), precision=lax.Precision.HIGHEST, preferred_element_type=jnp.float32) * (CLS / total)
        factor = jnp.linalg.cholesky(gram + ridge * jnp.eye(BLK, dtype=jnp.float32))
        solved = jax.scipy.linalg.cho_solve((factor, True), gradient)
        results.append(solved)
        residual = residual - jnp.dot(wide.astype(jnp.float32), solved.astype(jnp.float32), precision=lax.Precision.HIGHEST, preferred_element_type=jnp.float32) / CLS
    return (jnp.concatenate(results, axis=0), residual)
```

```python
import numpy as np
import jax
import jax.numpy as jnp
from jax import lax
from jax.experimental import pallas as pl
from jax.experimental.pallas import tpu as pltpu
from jax.sharding import Mesh, PartitionSpec as P

CLS = 1000
BLOCKS = 3
BLK = 512
SAMPLES = 32768
ROWS = 512
SHARE = 125
TILE = 128
LOCAL = 48
F32 = jnp.float32
BF16 = jnp.bfloat16
VMEM = pltpu.VMEM
VMEM_LIMIT = 56 << 20

DIAG = [(b, i, j) for b in range(BLOCKS) for i in range(4) for j in range(i + 1)]
CROSS = [(b, a, i, j) for b in range(BLOCKS) for a in range(b) for i in range(4) for j in range(4)]
DIAG_SLOTS, CROSS_SLOTS = 4, 6


def tile_tables():
    table = np.zeros((8, 2 * (DIAG_SLOTS + CROSS_SLOTS)), np.int32)
    for feat in range(8):
        pairs = []
        for slot in range(DIAG_SLOTS):
            b, i, j = DIAG[min(feat * DIAG_SLOTS + slot, len(DIAG) - 1)]
            pairs.append((b * 4 + i, b * 4 + j))
        for slot in range(CROSS_SLOTS):
            b, a, i, j = CROSS[feat * CROSS_SLOTS + slot]
            pairs.append((b * 4 + i, a * 4 + j))
        table[feat] = np.array(pairs, np.int32).reshape(-1)
    return table


def tap_places():
    places = np.zeros((108, 768), np.float32)
    for c in range(3):
        for a in range(6):
            for b in range(6):
                places[c * 36 + a * 6 + b, c * 256 + a * 32 + b] = 1.0
    return places


def full_specs(count):
    return [pl.BlockSpec(memory_space=VMEM)] * count


def dot_nt(left, right):
    return lax.dot_general(left, right, (((1,), (1,)), ((), ())), preferred_element_type=F32)


def dot_exact(left, right):
    return lax.dot_general(
        left, right, (((1,), (0,)), ((), ())), precision=lax.Precision.HIGHEST, preferred_element_type=F32
    )


def conv_kernel(x_ref, w_ref, place_ref, bias_ref, o_ref, taps, acc, mixed):
    base = lax.dot_general(
        w_ref[...], place_ref[...], (((1,), (0,)), ((), ())), preferred_element_type=F32
    )
    for p in range(2):
        for q in range(14):
            shift = 64 * p + 2 * q
            moved = base if shift == 0 else pltpu.roll(base, shift, 1)
            row = (p * 14 + q) * LOCAL
            taps[row : row + LOCAL, :] = moved.astype(BF16)
    acc[...] = jnp.zeros_like(acc)
    bias = jnp.broadcast_to(bias_ref[...], (LOCAL, ROWS))

    def step(t, carry):
        chunks = []
        for c in range(3):
            start = pl.multiple_of(c * 1024 + t * 128, 128)
            chunks.append(x_ref[:, pl.ds(start, 256)])
        pixels = jnp.concatenate(chunks, axis=1)
        for p in range(2):
            top = lax.select(2 * t + p >= 7, 2, 0)
            response = dot_nt(taps[p * 14 * LOCAL : (p + 1) * 14 * LOCAL, :], pixels)
            for j in range(2):
                total = None
                for q in range(7 * j, 7 * j + 7):
                    part = jnp.maximum(response[q * LOCAL : (q + 1) * LOCAL] + bias, 0.0)
                    total = part if total is None else total + part
                acc[top + j] += total
        return carry

    lax.fori_loop(0, 7, step, 0)
    for quadrant in range(4):
        for block in range(ROWS // TILE):
            lanes = slice(block * TILE, (block + 1) * TILE)
            mixed[block, pl.ds(quadrant, LOCAL, stride=4), :] = acc[quadrant, :, lanes] / 49.0
    for block in range(ROWS // TILE):
        o_ref[:, block * TILE : (block + 1) * TILE] = mixed[block].astype(BF16)


def local_features(images, weights, offsets):
    return pl.pallas_call(
        conv_kernel,
        out_shape=jax.ShapeDtypeStruct((4 * LOCAL, ROWS), BF16),
        in_specs=full_specs(4),
        out_specs=pl.BlockSpec(memory_space=VMEM),
        scratch_shapes=[
            VMEM((28 * LOCAL, 768), BF16),
            VMEM((4, LOCAL, ROWS), F32),
            VMEM((ROWS // TILE, 4 * LOCAL, TILE), F32),
        ],
        compiler_params=pltpu.CompilerParams(vmem_limit_bytes=VMEM_LIMIT),
        name="features",
    )(images, weights, jnp.asarray(tap_places(), BF16), offsets)


def products_kernel(feat_ref, table_ref, ft_ref, labels_ref, o_ref):
    feat = feat_ref[0]

    def tile(slot):
        left = pl.multiple_of(table_ref[feat, 2 * slot] * TILE, TILE)
        right = pl.multiple_of(table_ref[feat, 2 * slot + 1] * TILE, TILE)
        return dot_nt(ft_ref[pl.ds(left, TILE), :], ft_ref[pl.ds(right, TILE), :]).reshape(16, 8, TILE)

    for slot in range(DIAG_SLOTS):
        o_ref[16 * slot : 16 * slot + 16, 0:8, :] = tile(slot)
    for slot in range(8):
        unit, place = slot // 4, slot % 4
        value = tile(DIAG_SLOTS + slot) if slot < CROSS_SLOTS else jnp.zeros((16, 8, TILE), F32)
        o_ref[16 * place : 16 * place + 16, 8 + 8 * unit : 16 + 8 * unit, :] = value
    local_class = lax.broadcasted_iota(jnp.int32, (TILE, ROWS), 0)
    hit = (labels_ref[...] == local_class + feat * SHARE) & (local_class < SHARE)
    targets = jnp.where(hit, 1.0, 0.0).astype(BF16)
    for part in range(4):
        rows = slice(part * 384, (part + 1) * 384)
        o_ref[16 * part : 16 * part + 16, 24:48, :] = dot_nt(ft_ref[rows, :], targets).reshape(16, 24, TILE)


def local_products(feat, features, labels):
    return pl.pallas_call(
        products_kernel,
        out_shape=jax.ShapeDtypeStruct((64, 48, TILE), F32),
        in_specs=[pl.BlockSpec(memory_space=pltpu.SMEM)] * 2 + full_specs(2),
        out_specs=pl.BlockSpec(memory_space=VMEM),
        compiler_params=pltpu.CompilerParams(vmem_limit_bytes=VMEM_LIMIT),
        name="products",
    )(feat, jnp.asarray(tile_tables()), features, labels)


def small_inverse(columns, sub):
    for r in range(8):
        row = [jnp.broadcast_to(columns[j][r : r + 1, :], (8, TILE)) for j in range(8)]
        reciprocal = 1.0 / row[r]
        pivot = columns[r]
        following = []
        for j in range(8):
            if j == r:
                following.append(jnp.where(sub == r, reciprocal, -pivot * reciprocal))
            else:
                scaled = row[j] * reciprocal
                following.append(jnp.where(sub == r, scaled, columns[j] - pivot * scaled))
        columns = following
    return columns


def invert_tiles(work):
    count = work.shape[0]
    lane = lax.broadcasted_iota(jnp.int32, (8, TILE), 1)
    sub = lax.broadcasted_iota(jnp.int32, (8, TILE), 0)
    for k in range(16):
        low = 8 * k
        inside = (lane >= low) & (lane < low + 8)
        unit = jnp.where(lane == sub + low, 1.0, 0.0)
        for m in range(count):
            panel = work[m, k]
            columns = [jnp.broadcast_to(panel[:, low + j : low + j + 1], (8, TILE)) for j in range(8)]
            columns = small_inverse(columns, sub)
            source = jnp.where(inside, unit, panel)
            solved = None
            for j in range(8):
                term = columns[j] * jnp.broadcast_to(source[j : j + 1, :], (8, TILE))
                solved = term if solved is None else solved + term
            work[m, k] = solved
            rows = [jnp.broadcast_to(solved[j : j + 1, :], (8, TILE)) for j in range(8)]
            for i in range(16):
                if i == k:
                    continue
                value = work[m, i]
                total = jnp.where(inside, 0.0, value)
                for j in range(8):
                    total = total - jnp.broadcast_to(value[:, low + j : low + j + 1], (8, TILE)) * rows[j]
                work[m, i] = total


def inverse_kernel(core_ref, own_ref, other_ref, o_ref, grid, work):
    core = core_ref[0]
    eye = jnp.where(
        lax.broadcasted_iota(jnp.int32, (TILE, TILE), 0) == lax.broadcasted_iota(jnp.int32, (TILE, TILE), 1),
        1.0,
        0.0,
    )
    traces = [jnp.zeros((1, 1), F32)] * BLOCKS
    for place, (b, i, j) in enumerate(DIAG):
        feat, slot = place // DIAG_SLOTS, place % DIAG_SLOTS
        mine, theirs = own_ref[feat // 2, slot], other_ref[feat // 2, slot]
        tile = jnp.where(core == feat % 2, mine, theirs) * (1.0 / SAMPLES)
        grid[b, i, j] = tile
        if i != j:
            grid[b, j, i] = tile.T
        else:
            diagonal = jnp.sum(tile * eye, axis=1, keepdims=True)
            traces[b] = traces[b] + jnp.sum(diagonal, axis=0, keepdims=True)
    for b in range(BLOCKS):
        ridge = 0.1 * traces[b] / BLK + 1e-05
        for i in range(4):
            grid[b, i, i] += ridge * eye

    def pivot(k, carry):
        for b in range(BLOCKS):
            work[b] = grid[b, k, k].reshape(16, 8, TILE)
        invert_tiles(work)
        for b in range(BLOCKS):
            inverse = work[b].reshape(TILE, TILE)
            others = [lax.rem(k + d, 4) for d in (1, 2, 3)]
            for j in others:
                grid[b, k, j] = dot_exact(inverse, grid[b, k, j])
            for i in others:
                left = grid[b, i, k]
                for j in others:
                    grid[b, i, j] -= dot_exact(left, grid[b, k, j])
                grid[b, i, k] = -dot_exact(left, inverse)
            grid[b, k, k] = inverse
        return carry

    lax.fori_loop(0, 4, pivot, 0)
    for b in range(BLOCKS):
        for i in range(4):
            for j in range(4):
                o_ref[b, i * TILE : (i + 1) * TILE, j * TILE : (j + 1) * TILE] = grid[b, i, j]


def inverses(core, own, other):
    return pl.pallas_call(
        inverse_kernel,
        out_shape=jax.ShapeDtypeStruct((BLOCKS, BLK, BLK), F32),
        in_specs=[pl.BlockSpec(memory_space=pltpu.SMEM)] + full_specs(2),
        out_specs=pl.BlockSpec(memory_space=VMEM),
        scratch_shapes=[VMEM((BLOCKS, 4, 4, TILE, TILE), F32), VMEM((BLOCKS, 16, 8, TILE), F32)],
        compiler_params=pltpu.CompilerParams(vmem_limit_bytes=VMEM_LIMIT),
        cost_estimate=pl.CostEstimate(flops=9_000_000_000, bytes_accessed=100_000_000, transcendentals=0),
        name="inverses",
    )(core, own, other)


def solve_kernel(feat_ref, inverse_ref, cross_ref, fty_ref, ft_ref, labels_ref, coef_ref, res_ref, steps):
    for b in range(BLOCKS):
        gradient = fty_ref[b * BLK : (b + 1) * BLK, :] * (CLS / SAMPLES)
        for i in range(4):
            total = gradient[i * TILE : (i + 1) * TILE]
            for a in range(b):
                for j in range(4):
                    feat, slot = divmod(CROSS.index((b, a, i, j)), CROSS_SLOTS)
                    rows = slice(a * BLK + j * TILE, a * BLK + (j + 1) * TILE)
                    total = total - dot_exact(cross_ref[feat, slot] * (1.0 / SAMPLES), steps[rows, :])
            rows = slice(b * BLK + i * TILE, b * BLK + (i + 1) * TILE)
            steps[rows, :] = total
        rows = slice(b * BLK, (b + 1) * BLK)
        steps[rows, :] = dot_exact(inverse_ref[b], steps[rows, :])
    value = steps[...]
    coef_ref[...] = value[:, :SHARE]
    high = value.astype(BF16)
    rest = value - high.astype(F32)
    middle = rest.astype(BF16)
    low = (rest - middle.astype(F32)).astype(BF16)
    fit = None
    for part in (low, middle, high):
        term = lax.dot_general(ft_ref[...], part, (((0,), (0,)), ((), ())), preferred_element_type=F32)
        fit = term if fit is None else fit + term
    classes = lax.broadcasted_iota(jnp.int32, (ROWS, TILE), 1) + feat_ref[0] * SHARE
    targets = jnp.where(labels_ref[...] == classes, 1.0, 0.0)
    res_ref[...] = (targets - fit / CLS)[:, :SHARE]


def solve(feat, inverse, cross, fty, features, labels):
    return pl.pallas_call(
        solve_kernel,
        out_shape=(
            jax.ShapeDtypeStruct((BLOCKS * BLK, SHARE), F32),
            jax.ShapeDtypeStruct((ROWS, SHARE), F32),
        ),
        in_specs=[pl.BlockSpec(memory_space=pltpu.SMEM)] + full_specs(5),
        out_specs=(pl.BlockSpec(memory_space=VMEM), pl.BlockSpec(memory_space=VMEM)),
        scratch_shapes=[VMEM((BLOCKS * BLK, TILE), F32)],
        compiler_params=pltpu.CompilerParams(vmem_limit_bytes=VMEM_LIMIT),
        name="solve",
    )(feat, inverse, cross, fty, features, labels)


def gather_by_exchange(value, axis, size):
    copies = jnp.broadcast_to(value[None], (size,) + value.shape)
    return lax.all_to_all(copies, axis, 0, 0, tiled=True)


def swap_cores(value):
    return lax.ppermute(value, "c", [(0, 1), (1, 0)])


def per_device(images, labels, filters, biases):
    core = lax.axis_index("c")
    feat = (lax.axis_index("x") * 2 + core).reshape(1)
    core1 = core.reshape(1)
    panel = local_features(images, filters.reshape(LOCAL, 108), biases.reshape(LOCAL, 1))
    own = lax.all_gather(panel, "x", axis=0)
    other = swap_cores(own)
    pair = jnp.where(core == 0, jnp.stack([own, other]), jnp.stack([other, own]))
    features = pair.reshape(2, 4, BLOCKS, 64, ROWS).transpose(2, 1, 0, 3, 4).reshape(BLOCKS * BLK, ROWS)

    pieces = local_products(feat, features, labels.reshape(1, ROWS))
    pieces = lax.all_to_all(pieces.reshape(4, 16 * 48, TILE), "y", 0, 0, tiled=True)
    pieces = jnp.sum(pieces, axis=0).reshape(16, 48, TILE)
    pieces = jnp.sum(lax.all_to_all(pieces, "z", 0, 0, tiled=True), axis=0)
    column = gather_by_exchange(pieces, "z", 16)

    diagonal = lax.all_gather(column[:, :8], "y", axis=0).reshape(DIAG_SLOTS, TILE, TILE)
    diag_own = gather_by_exchange(diagonal, "x", 4)
    diag_other = swap_cores(diag_own)

    rest = lax.all_gather(column[:, 8:], "y", axis=0)
    rest, diag_own, diag_other = lax.optimization_barrier((rest, diag_own, diag_other))
    cross = rest[:, :, :16].reshape(64, 2, 8, TILE).transpose(1, 0, 2, 3).reshape(8, TILE, TILE)
    cross = lax.all_gather(cross[:CROSS_SLOTS], ("x", "c"), axis=0)
    fty = rest[:, :, 16:].reshape(BLOCKS * BLK, TILE)

    inverse = inverses(core1, diag_own, diag_other)
    return solve(feat, inverse, cross, fty, features, labels.reshape(ROWS, 1))


def solution(mesh):
    split = Mesh(mesh.devices.reshape(4, 16, 4, 2), ("y", "z", "x", "c"))
    samp, feat = ("y", "z"), ("x", "c")
    return jax.shard_map(
        per_device,
        mesh=split,
        in_specs=(P(samp, None), P(samp), P(None, feat, None), P(None, feat)),
        out_specs=(P(None, feat), P(samp, feat)),
        check_vma=False,
    )
```

```python
import numpy as np
import jax
import jax.numpy as jnp
from jax import lax
from jax.experimental import pallas as pl
from jax.experimental.pallas import tpu as pltpu
from jax.sharding import Mesh, PartitionSpec as P

CLS = 1000
BLOCKS = 3
BLK = 512
SAMPLES = 32768
ROWS = 512
SHARE = 125
TILE = 128
LOCAL = 48
F32 = jnp.float32
BF16 = jnp.bfloat16
VMEM = pltpu.VMEM
VMEM_LIMIT = 56 << 20

DIAG = [(b, i, j) for b in range(BLOCKS) for i in range(4) for j in range(i + 1)]
CROSS = [(b, a, i, j) for b in range(BLOCKS) for a in range(b) for i in range(4) for j in range(4)]
DIAG_SLOTS, CROSS_SLOTS = 4, 6
LOWER = [(i, j) for i in range(4) for j in range(i)]
PANEL = 32


def tile_tables():
    table = np.zeros((8, 2 * (DIAG_SLOTS + CROSS_SLOTS)), np.int32)
    for feat in range(8):
        pairs = []
        for slot in range(DIAG_SLOTS):
            b, i, j = DIAG[min(feat * DIAG_SLOTS + slot, len(DIAG) - 1)]
            pairs.append((b * 4 + i, b * 4 + j))
        for slot in range(CROSS_SLOTS):
            b, a, i, j = CROSS[feat * CROSS_SLOTS + slot]
            pairs.append((b * 4 + i, a * 4 + j))
        table[feat] = np.array(pairs, np.int32).reshape(-1)
    return table


def tap_places():
    places = np.zeros((108, 768), np.float32)
    for c in range(3):
        for a in range(6):
            for b in range(6):
                places[c * 36 + a * 6 + b, c * 256 + a * 32 + b] = 1.0
    return places


def full_specs(count):
    return [pl.BlockSpec(memory_space=VMEM)] * count


def dot_nt(left, right):
    return lax.dot_general(left, right, (((1,), (1,)), ((), ())), preferred_element_type=F32)


def exact(left, right, over):
    return lax.dot_general(
        left, right, (over, ((), ())), precision=lax.Precision.HIGHEST, preferred_element_type=F32
    )


def dot_exact(left, right):
    return exact(left, right, ((1,), (0,)))


def dot_nt_exact(left, right):
    return exact(left, right, ((1,), (1,)))


def dot_tn_exact(left, right):
    return exact(left, right, ((0,), (0,)))


def conv_kernel(x_ref, w_ref, place_ref, bias_ref, o_ref, taps, acc, mixed):
    base = lax.dot_general(
        w_ref[...], place_ref[...], (((1,), (0,)), ((), ())), preferred_element_type=F32
    )
    for p in range(2):
        for q in range(14):
            shift = 64 * p + 2 * q
            moved = base if shift == 0 else pltpu.roll(base, shift, 1)
            row = (p * 14 + q) * LOCAL
            taps[row : row + LOCAL, :] = moved.astype(BF16)
    acc[...] = jnp.zeros_like(acc)
    square = (16, 16)
    unit = lax.broadcasted_iota(jnp.int32, square, 0) == lax.broadcasted_iota(jnp.int32, square, 1)
    spread = [jnp.broadcast_to(bias_ref[b : b + 1, :], square) for b in range(BLOCKS)]
    upright = [jnp.sum(jnp.where(unit, rows, 0.0), axis=1, keepdims=True) for rows in spread]
    bias = jnp.broadcast_to(jnp.concatenate(upright, axis=0), (LOCAL, ROWS))

    def step(t, carry):
        chunks = []
        for c in range(3):
            start = pl.multiple_of(c * 1024 + t * 128, 128)
            chunks.append(x_ref[:, pl.ds(start, 256)])
        pixels = jnp.concatenate(chunks, axis=1)
        for p in range(2):
            top = lax.select(2 * t + p >= 7, 2, 0)
            response = dot_nt(taps[p * 14 * LOCAL : (p + 1) * 14 * LOCAL, :], pixels)
            for j in range(2):
                total = None
                for q in range(7 * j, 7 * j + 7):
                    part = jnp.maximum(response[q * LOCAL : (q + 1) * LOCAL] + bias, 0.0)
                    total = part if total is None else total + part
                acc[top + j] += total
        return carry

    lax.fori_loop(0, 7, step, 0)
    for quadrant in range(4):
        for block in range(ROWS // TILE):
            lanes = slice(block * TILE, (block + 1) * TILE)
            mixed[block, pl.ds(quadrant, LOCAL, stride=4), :] = acc[quadrant, :, lanes] / 49.0
    for block in range(ROWS // TILE):
        o_ref[:, block * TILE : (block + 1) * TILE] = mixed[block].astype(BF16)


def local_features(images, weights, offsets):
    return pl.pallas_call(
        conv_kernel,
        out_shape=jax.ShapeDtypeStruct((4 * LOCAL, ROWS), BF16),
        in_specs=full_specs(4),
        out_specs=pl.BlockSpec(memory_space=VMEM),
        scratch_shapes=[
            VMEM((28 * LOCAL, 768), BF16),
            VMEM((4, LOCAL, ROWS), F32),
            VMEM((ROWS // TILE, 4 * LOCAL, TILE), F32),
        ],
        compiler_params=pltpu.CompilerParams(vmem_limit_bytes=VMEM_LIMIT),
        name="features",
    )(images, weights, jnp.asarray(tap_places(), BF16), offsets)


def products_kernel(feat_ref, table_ref, ft_ref, labels_ref, o_ref):
    feat = feat_ref[0]

    def tile(slot):
        left = pl.multiple_of(table_ref[feat, 2 * slot] * TILE, TILE)
        right = pl.multiple_of(table_ref[feat, 2 * slot + 1] * TILE, TILE)
        return dot_nt(ft_ref[pl.ds(left, TILE), :], ft_ref[pl.ds(right, TILE), :]).reshape(16, 8, TILE)

    for slot in range(DIAG_SLOTS):
        o_ref[16 * slot : 16 * slot + 16, 0:8, :] = tile(slot)
    for slot in range(8):
        unit, place = slot // 4, slot % 4
        value = tile(DIAG_SLOTS + slot) if slot < CROSS_SLOTS else jnp.zeros((16, 8, TILE), F32)
        o_ref[16 * place : 16 * place + 16, 8 + 8 * unit : 16 + 8 * unit, :] = value
    local_class = lax.broadcasted_iota(jnp.int32, (TILE, ROWS), 0)
    hit = (labels_ref[...] == local_class + feat * SHARE) & (local_class < SHARE)
    targets = jnp.where(hit, 1.0, 0.0).astype(BF16)
    for part in range(4):
        rows = slice(part * 384, (part + 1) * 384)
        o_ref[16 * part : 16 * part + 16, 24:48, :] = dot_nt(ft_ref[rows, :], targets).reshape(16, 24, TILE)


def local_products(feat, features, labels):
    return pl.pallas_call(
        products_kernel,
        out_shape=jax.ShapeDtypeStruct((64, 48, TILE), F32),
        in_specs=[pl.BlockSpec(memory_space=pltpu.SMEM)] * 2 + full_specs(2),
        out_specs=pl.BlockSpec(memory_space=VMEM),
        compiler_params=pltpu.CompilerParams(vmem_limit_bytes=VMEM_LIMIT),
        name="products",
    )(feat, jnp.asarray(tile_tables()), features, labels)


def along_lanes(value, j):
    return jnp.broadcast_to(value[:, j : j + 1], (8, TILE))


def along_rows(value, j):
    return jnp.broadcast_to(value[j : j + 1, :], (8, TILE))


def add_up(terms):
    while len(terms) > 1:
        paired = [terms[i] + terms[i + 1] for i in range(0, len(terms) - 1, 2)]
        terms = paired + ([terms[-1]] if len(terms) % 2 else [])
    return terms[0]


def small_inverses(columns, sub):
    count = len(columns)
    for r in range(8):
        here = sub == r
        rows = [[along_rows(columns[m][j], r) for j in range(8)] for m in range(count)]
        reciprocals = [1.0 / rows[m][r] for m in range(count)]
        following = [[None] * 8 for _ in range(count)]
        for j in range(8):
            for m in range(count):
                pivot = columns[m][r]
                if j == r:
                    following[m][j] = jnp.where(here, reciprocals[m], -pivot * reciprocals[m])
                else:
                    scaled = rows[m][j] * reciprocals[m]
                    following[m][j] = jnp.where(here, scaled, columns[m][j] - pivot * scaled)
        columns = following
    return columns


def invert_tiles(work):
    count = work.shape[0]
    lane = lax.broadcasted_iota(jnp.int32, (8, TILE), 1)
    sub = lax.broadcasted_iota(jnp.int32, (8, TILE), 0)
    wide_lane = lax.broadcasted_iota(jnp.int32, (TILE, TILE), 1)
    for start in range(0, TILE, PANEL):
        first, steps = start // 8, PANEL // 8
        whole = [work[m].reshape(TILE, TILE) for m in range(count)]
        panels = [[work[m, first + i] for i in range(steps)] for m in range(count)]
        for k in range(steps):
            low = start + 8 * k
            inside = (lane >= low) & (lane < low + 8)
            unit = jnp.where(lane == sub + low, 1.0, 0.0)
            inverted = small_inverses(
                [[along_lanes(panels[m][k], low + j) for j in range(8)] for m in range(count)], sub
            )
            sources = [jnp.where(inside, unit, panels[m][k]) for m in range(count)]
            solved = [
                add_up([inverted[m][j] * along_rows(sources[m], j) for j in range(8)]) for m in range(count)
            ]
            rows = [[along_rows(solved[m], j) for j in range(8)] for m in range(count)]
            following = [[None] * steps for _ in range(count)]
            for d in range(steps):
                i = (k + d) % steps
                for m in range(count):
                    if d == 0:
                        following[m][i] = solved[m]
                        continue
                    value = panels[m][i]
                    change = add_up([along_lanes(value, low + j) * rows[m][j] for j in range(8)])
                    following[m][i] = jnp.where(inside, 0.0, value) - change
            panels = following
        inside = (wide_lane >= start) & (wide_lane < start + PANEL)
        for m in range(count):
            change = dot_exact(whole[m][:, start : start + PANEL], jnp.concatenate(panels[m], axis=0))
            work[m] = (jnp.where(inside, 0.0, whole[m]) - change).reshape(16, 8, TILE)
            for i in range(steps):
                work[m, first + i] = panels[m][i]


def factor_kernel(core_ref, own_ref, other_ref, pivot_ref, lower_ref, grid, work):
    core = core_ref[0]
    eye = jnp.where(
        lax.broadcasted_iota(jnp.int32, (TILE, TILE), 0) == lax.broadcasted_iota(jnp.int32, (TILE, TILE), 1),
        1.0,
        0.0,
    )
    traces = [jnp.zeros((1, 1), F32)] * BLOCKS
    for place, (b, i, j) in enumerate(DIAG):
        feat, slot = place // DIAG_SLOTS, place % DIAG_SLOTS
        mine, theirs = own_ref[slot, feat // 2], other_ref[slot, feat // 2]
        tile = jnp.where(core == feat % 2, mine, theirs) * (1.0 / SAMPLES)
        grid[b, i, j] = tile
        if i == j:
            diagonal = jnp.sum(tile * eye, axis=1, keepdims=True)
            traces[b] = traces[b] + jnp.sum(diagonal, axis=0, keepdims=True)
    for b in range(BLOCKS):
        ridge = 0.1 * traces[b] / BLK + 1e-05
        for i in range(4):
            grid[b, i, i] += ridge * eye

    for k in range(4):
        for b in range(BLOCKS):
            work[b] = grid[b, k, k].reshape(16, 8, TILE)
        invert_tiles(work)
        inverse = [work[b].reshape(TILE, TILE) for b in range(BLOCKS)]
        factors = {}
        for i in range(k + 1, 4):
            for b in range(BLOCKS):
                factors[b, i] = dot_exact(grid[b, i, k], inverse[b])
            for j in range(k + 1, i + 1):
                for b in range(BLOCKS):
                    grid[b, i, j] -= dot_nt_exact(factors[b, i], grid[b, j, k])
        for b in range(BLOCKS):
            pivot_ref[b, k] = inverse[b]
        for i in range(k + 1, 4):
            for b in range(BLOCKS):
                for j in range(k):
                    lower_ref[b, LOWER.index((i, j))] -= dot_exact(factors[b, i], lower_ref[b, LOWER.index((k, j))])
                lower_ref[b, LOWER.index((i, k))] = -factors[b, i]


def factor(core, own, other):
    return pl.pallas_call(
        factor_kernel,
        out_shape=(
            jax.ShapeDtypeStruct((BLOCKS, 4, TILE, TILE), F32),
            jax.ShapeDtypeStruct((BLOCKS, len(LOWER), TILE, TILE), F32),
        ),
        in_specs=[pl.BlockSpec(memory_space=pltpu.SMEM)] + full_specs(2),
        out_specs=(pl.BlockSpec(memory_space=VMEM), pl.BlockSpec(memory_space=VMEM)),
        scratch_shapes=[VMEM((BLOCKS, 4, 4, TILE, TILE), F32), VMEM((BLOCKS, 16, 8, TILE), F32)],
        compiler_params=pltpu.CompilerParams(vmem_limit_bytes=VMEM_LIMIT),
        cost_estimate=pl.CostEstimate(flops=9_000_000_000, bytes_accessed=100_000_000, transcendentals=0),
        name="factor",
    )(core, own, other)


def solve_kernel(feat_ref, pivot_ref, lower_ref, cross_ref, rest_ref, ft_ref, labels_ref, coef_ref, res_ref, steps):
    fit = jnp.zeros((ROWS, TILE), F32)
    for b in range(BLOCKS):
        block = slice(b * BLK, (b + 1) * BLK)
        parts = []
        gradient = rest_ref[b * 64 // 3 : b * 64 // 3 + 22, 16:40, :].reshape(22 * 24, TILE)
        gradient = gradient[b * BLK - b * 64 // 3 * 24 :][:BLK] * (CLS / SAMPLES)
        for i in range(4):
            total = gradient[i * TILE : (i + 1) * TILE]
            for a in range(b):
                tiles = []
                for j in range(4):
                    feat, slot = divmod(CROSS.index((b, a, i, j)), CROSS_SLOTS)
                    tiles.append(cross_ref[feat, slot])
                strip = jnp.concatenate(tiles, axis=1) * (1.0 / SAMPLES)
                total = total - dot_exact(strip, steps[a * BLK : (a + 1) * BLK, :])
            parts.append(total)
        forward = []
        for i in range(4):
            total = parts[i]
            if i:
                strip = jnp.concatenate([lower_ref[b, LOWER.index((i, j))] for j in range(i)], axis=1)
                total = total + dot_exact(strip, jnp.concatenate(parts[:i], axis=0))
            forward.append(dot_exact(pivot_ref[b, i], total))
        for i in range(4):
            total = forward[i]
            if i < 3:
                strip = jnp.concatenate([lower_ref[b, LOWER.index((j, i))] for j in range(i + 1, 4)], axis=0)
                total = total + dot_tn_exact(strip, jnp.concatenate(forward[i + 1 :], axis=0))
            steps[b * BLK + i * TILE : b * BLK + (i + 1) * TILE, :] = total
        value = steps[block, :]
        coef_ref[block, :] = value[:, :SHARE]
        high = value.astype(BF16)
        left = value - high.astype(F32)
        middle = left.astype(BF16)
        low = (left - middle.astype(F32)).astype(BF16)
        terms = lax.dot_general(
            ft_ref[block, :],
            jnp.concatenate([high, middle, low], axis=1),
            (((0,), (0,)), ((), ())),
            preferred_element_type=F32,
        )
        fit = fit + ((terms[:, 2 * TILE :] + terms[:, TILE : 2 * TILE]) + terms[:, :TILE])
    local = (labels_ref[...] - feat_ref[0] * SHARE).astype(F32)
    upright = jnp.broadcast_to(local, (TILE, ROWS)).T
    classes = lax.broadcasted_iota(jnp.int32, (ROWS, TILE), 1).astype(F32)
    targets = jnp.where(upright == classes, 1.0, 0.0)
    res_ref[...] = (targets - fit / CLS)[:, :SHARE]


def solve(feat, pivots, lower, cross, rest, features, labels):
    return pl.pallas_call(
        solve_kernel,
        out_shape=(
            jax.ShapeDtypeStruct((BLOCKS * BLK, SHARE), F32),
            jax.ShapeDtypeStruct((ROWS, SHARE), F32),
        ),
        in_specs=[pl.BlockSpec(memory_space=pltpu.SMEM)] + full_specs(6),
        out_specs=(pl.BlockSpec(memory_space=VMEM), pl.BlockSpec(memory_space=VMEM)),
        scratch_shapes=[VMEM((BLOCKS * BLK, TILE), F32)],
        compiler_params=pltpu.CompilerParams(vmem_limit_bytes=VMEM_LIMIT),
        name="solve",
    )(feat, pivots, lower, cross, rest, features, labels)


def gather_by_exchange(value, axis, size):
    copies = jnp.broadcast_to(value[None], (size,) + value.shape)
    return lax.all_to_all(copies, axis, 0, 0, tiled=True)


def swap_cores(value):
    return lax.ppermute(value, "c", [(0, 1), (1, 0)])


def per_device(images, labels, filters, biases):
    core = lax.axis_index("c")
    feat = (lax.axis_index("x") * 2 + core).reshape(1)
    core1 = core.reshape(1)
    panel = local_features(images, filters.reshape(LOCAL, 108), biases)
    own = lax.all_gather(panel, "x", axis=0)
    other = swap_cores(own)
    pair = jnp.where(core == 0, jnp.stack([own, other]), jnp.stack([other, own]))
    features = pair.reshape(2, 4, BLOCKS, 64, ROWS).transpose(2, 1, 0, 3, 4).reshape(BLOCKS * BLK, ROWS)

    pieces = local_products(feat, features, labels.reshape(1, ROWS))
    pieces = lax.all_to_all(pieces.reshape(4, 16 * 48, TILE), "y", 0, 0, tiled=True)
    pieces = jnp.sum(pieces, axis=0).reshape(16, 48, TILE)
    pieces = jnp.sum(lax.all_to_all(pieces, "z", 0, 0, tiled=True), axis=0)
    column = gather_by_exchange(pieces, "z", 16)

    diag_own = gather_by_exchange(column[:, :8], ("y", "x"), 16).reshape(DIAG_SLOTS, 4, TILE, TILE)
    diag_other = swap_cores(diag_own)

    rest = lax.all_gather(column[:, 8:], "y", axis=0)
    rest, diag_own, diag_other = lax.optimization_barrier((rest, diag_own, diag_other))
    rest = rest.reshape(64, 40, TILE)
    cross = jnp.concatenate([rest[:, 0:8], rest[:32, 8:16]], axis=0).reshape(CROSS_SLOTS, TILE, TILE)
    cross = lax.all_gather(cross, ("x", "c"), axis=0)

    pivots, lower = factor(core1, diag_own, diag_other)
    return solve(feat, pivots, lower, cross, rest, features, labels.reshape(1, ROWS))


def solution(mesh):
    split = Mesh(mesh.devices.reshape(4, 16, 4, 2), ("y", "z", "x", "c"))
    samp, feat = ("y", "z"), ("x", "c")
    return jax.shard_map(
        per_device,
        mesh=split,
        in_specs=(P(samp, None), P(samp), P(None, feat, None), P(None, feat)),
        out_specs=(P(None, feat), P(samp, feat)),
        check_vma=False,
    )
```

```python
import numpy as np
import jax
import jax.numpy as jnp
from jax import lax
from jax.experimental import pallas as pl
from jax.experimental.pallas import tpu as pltpu
from jax.sharding import Mesh, PartitionSpec as P

CLS = 1000
BLOCKS = 3
BLK = 512
SAMPLES = 32768
ROWS = 512
SHARE = 125
TILE = 128
LOCAL = 48
F32 = jnp.float32
BF16 = jnp.bfloat16
VMEM = pltpu.VMEM
VMEM_LIMIT = 56 << 20

DIAG = [(b, i, j) for b in range(BLOCKS) for i in range(4) for j in range(i + 1)]
CROSS = [(b, a, i, j) for b in range(BLOCKS) for a in range(b) for i in range(4) for j in range(4)]
DIAG_SLOTS, CROSS_SLOTS = 4, 6
LOWER = [(i, j) for i in range(4) for j in range(i)]
PANEL = 32


def tile_tables():
    table = np.zeros((8, 2 * (DIAG_SLOTS + CROSS_SLOTS)), np.int32)
    for feat in range(8):
        pairs = []
        for slot in range(DIAG_SLOTS):
            b, i, j = DIAG[min(feat * DIAG_SLOTS + slot, len(DIAG) - 1)]
            pairs.append((b * 4 + i, b * 4 + j))
        for slot in range(CROSS_SLOTS):
            b, a, i, j = CROSS[feat * CROSS_SLOTS + slot]
            pairs.append((b * 4 + i, a * 4 + j))
        table[feat] = np.array(pairs, np.int32).reshape(-1)
    return table


def tap_places():
    places = np.zeros((108, 768), np.float32)
    for c in range(3):
        for a in range(6):
            for b in range(6):
                places[c * 36 + a * 6 + b, c * 256 + a * 32 + b] = 1.0
    return places


def full_specs(count):
    return [pl.BlockSpec(memory_space=VMEM)] * count


def dot_nt(left, right):
    return lax.dot_general(left, right, (((1,), (1,)), ((), ())), preferred_element_type=F32)


def exact(left, right, over):
    return lax.dot_general(
        left, right, (over, ((), ())), precision=lax.Precision.HIGHEST, preferred_element_type=F32
    )


def dot_exact(left, right):
    return exact(left, right, ((1,), (0,)))


def dot_nt_exact(left, right):
    return exact(left, right, ((1,), (1,)))


def dot_tn_exact(left, right):
    return exact(left, right, ((0,), (0,)))


def conv_kernel(x_ref, w_ref, place_ref, bias_ref, o_ref, taps, acc, mixed):
    base = lax.dot_general(
        w_ref[...], place_ref[...], (((1,), (0,)), ((), ())), preferred_element_type=F32
    )
    for p in range(2):
        for q in range(14):
            shift = 64 * p + 2 * q
            moved = base if shift == 0 else pltpu.roll(base, shift, 1)
            row = (p * 14 + q) * LOCAL
            taps[row : row + LOCAL, :] = moved.astype(BF16)
    acc[...] = jnp.zeros_like(acc)
    square = (16, 16)
    unit = lax.broadcasted_iota(jnp.int32, square, 0) == lax.broadcasted_iota(jnp.int32, square, 1)
    spread = [jnp.broadcast_to(bias_ref[b : b + 1, :], square) for b in range(BLOCKS)]
    upright = [jnp.sum(jnp.where(unit, rows, 0.0), axis=1, keepdims=True) for rows in spread]
    bias = jnp.broadcast_to(jnp.concatenate(upright, axis=0), (LOCAL, ROWS))

    def step(t, carry):
        chunks = []
        for c in range(3):
            start = pl.multiple_of(c * 1024 + t * 128, 128)
            chunks.append(x_ref[:, pl.ds(start, 256)])
        pixels = jnp.concatenate(chunks, axis=1)
        for p in range(2):
            top = lax.select(2 * t + p >= 7, 2, 0)
            response = dot_nt(taps[p * 14 * LOCAL : (p + 1) * 14 * LOCAL, :], pixels)
            for j in range(2):
                total = None
                for q in range(7 * j, 7 * j + 7):
                    part = jnp.maximum(response[q * LOCAL : (q + 1) * LOCAL] + bias, 0.0)
                    total = part if total is None else total + part
                acc[top + j] += total
        return carry

    lax.fori_loop(0, 7, step, 0)
    for quadrant in range(4):
        for block in range(ROWS // TILE):
            lanes = slice(block * TILE, (block + 1) * TILE)
            mixed[block, pl.ds(quadrant, LOCAL, stride=4), :] = acc[quadrant, :, lanes] / 49.0
    for block in range(ROWS // TILE):
        o_ref[:, block * TILE : (block + 1) * TILE] = mixed[block].astype(BF16)


def local_features(images, weights, offsets):
    return pl.pallas_call(
        conv_kernel,
        out_shape=jax.ShapeDtypeStruct((4 * LOCAL, ROWS), BF16),
        in_specs=full_specs(4),
        out_specs=pl.BlockSpec(memory_space=VMEM),
        scratch_shapes=[
            VMEM((28 * LOCAL, 768), BF16),
            VMEM((4, LOCAL, ROWS), F32),
            VMEM((ROWS // TILE, 4 * LOCAL, TILE), F32),
        ],
        compiler_params=pltpu.CompilerParams(vmem_limit_bytes=VMEM_LIMIT),
        name="features",
    )(images, weights, jnp.asarray(tap_places(), BF16), offsets)


def products_kernel(feat_ref, table_ref, ft_ref, labels_ref, o_ref):
    feat = feat_ref[0]

    def tile(slot):
        left = pl.multiple_of(table_ref[feat, 2 * slot] * TILE, TILE)
        right = pl.multiple_of(table_ref[feat, 2 * slot + 1] * TILE, TILE)
        return dot_nt(ft_ref[pl.ds(left, TILE), :], ft_ref[pl.ds(right, TILE), :]).reshape(16, 8, TILE)

    for slot in range(DIAG_SLOTS):
        o_ref[16 * slot : 16 * slot + 16, 0:8, :] = tile(slot)
    for slot in range(8):
        unit, place = slot // 4, slot % 4
        value = tile(DIAG_SLOTS + slot) if slot < CROSS_SLOTS else jnp.zeros((16, 8, TILE), F32)
        o_ref[16 * place : 16 * place + 16, 8 + 8 * unit : 16 + 8 * unit, :] = value
    local_class = lax.broadcasted_iota(jnp.int32, (TILE, ROWS), 0)
    hit = (labels_ref[...] == local_class + feat * SHARE) & (local_class < SHARE)
    targets = jnp.where(hit, 1.0, 0.0).astype(BF16)
    for part in range(4):
        rows = slice(part * 384, (part + 1) * 384)
        o_ref[16 * part : 16 * part + 16, 24:48, :] = dot_nt(ft_ref[rows, :], targets).reshape(16, 24, TILE)


def local_products(feat, features, labels):
    return pl.pallas_call(
        products_kernel,
        out_shape=jax.ShapeDtypeStruct((64, 48, TILE), F32),
        in_specs=[pl.BlockSpec(memory_space=pltpu.SMEM)] * 2 + full_specs(2),
        out_specs=pl.BlockSpec(memory_space=VMEM),
        compiler_params=pltpu.CompilerParams(vmem_limit_bytes=VMEM_LIMIT),
        name="products",
    )(feat, jnp.asarray(tile_tables()), features, labels)


def along_lanes(value, j):
    return jnp.broadcast_to(value[:, j : j + 1], (8, TILE))


def along_rows(value, j):
    return jnp.broadcast_to(value[j : j + 1, :], (8, TILE))


def add_up(terms):
    while len(terms) > 1:
        paired = [terms[i] + terms[i + 1] for i in range(0, len(terms) - 1, 2)]
        terms = paired + ([terms[-1]] if len(terms) % 2 else [])
    return terms[0]


def small_inverses(columns, sub):
    count = len(columns)
    for r in range(8):
        here = sub == r
        rows = [[along_rows(columns[m][j], r) for j in range(8)] for m in range(count)]
        reciprocals = [1.0 / rows[m][r] for m in range(count)]
        following = [[None] * 8 for _ in range(count)]
        for j in range(8):
            for m in range(count):
                pivot = columns[m][r]
                if j == r:
                    following[m][j] = jnp.where(here, reciprocals[m], -pivot * reciprocals[m])
                else:
                    scaled = rows[m][j] * reciprocals[m]
                    following[m][j] = jnp.where(here, scaled, columns[m][j] - pivot * scaled)
        columns = following
    return columns


def invert_tiles(work):
    count = work.shape[0]
    lane = lax.broadcasted_iota(jnp.int32, (8, TILE), 1)
    sub = lax.broadcasted_iota(jnp.int32, (8, TILE), 0)
    wide_lane = lax.broadcasted_iota(jnp.int32, (TILE, TILE), 1)
    for start in range(0, TILE, PANEL):
        first, steps = start // 8, PANEL // 8
        whole = [work[m].reshape(TILE, TILE) for m in range(count)]
        panels = [[work[m, first + i] for i in range(steps)] for m in range(count)]
        for k in range(steps):
            low = start + 8 * k
            inside = (lane >= low) & (lane < low + 8)
            unit = jnp.where(lane == sub + low, 1.0, 0.0)
            inverted = small_inverses(
                [[along_lanes(panels[m][k], low + j) for j in range(8)] for m in range(count)], sub
            )
            sources = [jnp.where(inside, unit, panels[m][k]) for m in range(count)]
            solved = [
                add_up([inverted[m][j] * along_rows(sources[m], j) for j in range(8)]) for m in range(count)
            ]
            rows = [[along_rows(solved[m], j) for j in range(8)] for m in range(count)]
            following = [[None] * steps for _ in range(count)]
            for d in range(steps):
                i = (k + d) % steps
                for m in range(count):
                    if d == 0:
                        following[m][i] = solved[m]
                        continue
                    value = panels[m][i]
                    change = add_up([along_lanes(value, low + j) * rows[m][j] for j in range(8)])
                    following[m][i] = jnp.where(inside, 0.0, value) - change
            panels = following
        inside = (wide_lane >= start) & (wide_lane < start + PANEL)
        for m in range(count):
            change = dot_exact(whole[m][:, start : start + PANEL], jnp.concatenate(panels[m], axis=0))
            work[m] = (jnp.where(inside, 0.0, whole[m]) - change).reshape(16, 8, TILE)
            for i in range(steps):
                work[m, first + i] = panels[m][i]


def factor_kernel(core_ref, own_ref, other_ref, pivot_ref, lower_ref, last_ref, grid, work):
    core = core_ref[0]
    eye = jnp.where(
        lax.broadcasted_iota(jnp.int32, (TILE, TILE), 0) == lax.broadcasted_iota(jnp.int32, (TILE, TILE), 1),
        1.0,
        0.0,
    )
    traces = [jnp.zeros((1, 1), F32)] * BLOCKS
    for place, (b, i, j) in enumerate(DIAG):
        feat, slot = place // DIAG_SLOTS, place % DIAG_SLOTS
        mine, theirs = own_ref[slot, feat // 2], other_ref[slot, feat // 2]
        tile = jnp.where(core == feat % 2, mine, theirs) * (1.0 / SAMPLES)
        grid[b, i, j] = tile
        if i == j:
            diagonal = jnp.sum(tile * eye, axis=1, keepdims=True)
            traces[b] = traces[b] + jnp.sum(diagonal, axis=0, keepdims=True)
    for b in range(BLOCKS):
        ridge = 0.1 * traces[b] / BLK + 1e-05
        for i in range(4):
            grid[b, i, i] += ridge * eye

    for k in range(3):
        for b in range(BLOCKS):
            work[b] = grid[b, k, k].reshape(16, 8, TILE)
        invert_tiles(work)
        inverse = [work[b].reshape(TILE, TILE) for b in range(BLOCKS)]
        factors = {}
        for i in range(k + 1, 4):
            for b in range(BLOCKS):
                factors[b, i] = dot_exact(grid[b, i, k], inverse[b])
            for j in range(k + 1, i + 1):
                for b in range(BLOCKS):
                    grid[b, i, j] -= dot_nt_exact(factors[b, i], grid[b, j, k])
        for b in range(BLOCKS):
            pivot_ref[b, k] = inverse[b]
        for i in range(k + 1, 4):
            for b in range(BLOCKS):
                for j in range(k):
                    lower_ref[b, LOWER.index((i, j))] -= dot_exact(factors[b, i], lower_ref[b, LOWER.index((k, j))])
                lower_ref[b, LOWER.index((i, k))] = -factors[b, i]
    for b in range(BLOCKS):
        last_ref[b] = grid[b, 3, 3].reshape(16, 8, TILE)


def last_kernel(last_ref, o_ref, work):
    work[...] = last_ref[...]
    invert_tiles(work)
    o_ref[...] = work[...].reshape(BLOCKS, TILE, TILE)


def last_pivots(last):
    return pl.pallas_call(
        last_kernel,
        out_shape=jax.ShapeDtypeStruct((BLOCKS, TILE, TILE), F32),
        in_specs=full_specs(1),
        out_specs=pl.BlockSpec(memory_space=VMEM),
        scratch_shapes=[VMEM((BLOCKS, 16, 8, TILE), F32)],
        compiler_params=pltpu.CompilerParams(vmem_limit_bytes=VMEM_LIMIT),
        cost_estimate=pl.CostEstimate(flops=5_000_000_000, bytes_accessed=10_000_000, transcendentals=0),
        name="last_pivots",
    )(last)


def factor(core, own, other):
    return pl.pallas_call(
        factor_kernel,
        out_shape=(
            jax.ShapeDtypeStruct((BLOCKS, 3, TILE, TILE), F32),
            jax.ShapeDtypeStruct((BLOCKS, len(LOWER), TILE, TILE), F32),
            jax.ShapeDtypeStruct((BLOCKS, 16, 8, TILE), F32),
        ),
        in_specs=[pl.BlockSpec(memory_space=pltpu.SMEM)] + full_specs(2),
        out_specs=(pl.BlockSpec(memory_space=VMEM),) * 3,
        scratch_shapes=[VMEM((BLOCKS, 4, 4, TILE, TILE), F32), VMEM((BLOCKS, 16, 8, TILE), F32)],
        compiler_params=pltpu.CompilerParams(vmem_limit_bytes=VMEM_LIMIT),
        cost_estimate=pl.CostEstimate(flops=25_000_000_000, bytes_accessed=50_000_000, transcendentals=0),
        name="factor",
    )(core, own, other)


def solve_kernel(
    feat_ref, pivot_ref, last_ref, lower_ref, own_ref, other_ref, rest_ref, ft_ref, labels_ref, coef_ref, res_ref, steps
):
    core = lax.rem(feat_ref[0], 2)
    fit = jnp.zeros((ROWS, TILE), F32)
    for b in range(BLOCKS):
        block = slice(b * BLK, (b + 1) * BLK)
        parts = []
        gradient = rest_ref[b * 64 // 3 : b * 64 // 3 + 22, 8:32, :].reshape(22 * 24, TILE)
        gradient = gradient[b * BLK - b * 64 // 3 * 24 :][:BLK] * (CLS / SAMPLES)
        for i in range(4):
            total = gradient[i * TILE : (i + 1) * TILE]
            for a in range(b):
                tiles = []
                for j in range(4):
                    feat, slot = divmod(CROSS.index((b, a, i, j)), CROSS_SLOTS)
                    place = (slot % 4, feat // 2, slice(None), slice(8 * (slot // 4), 8 * (slot // 4) + 8))
                    tile = jnp.where(core == feat % 2, own_ref[place], other_ref[place])
                    tiles.append(tile.reshape(TILE, TILE))
                strip = jnp.concatenate(tiles, axis=1) * (1.0 / SAMPLES)
                total = total - dot_exact(strip, steps[a * BLK : (a + 1) * BLK, :])
            parts.append(total)
        forward = []
        for i in range(4):
            total = parts[i]
            if i:
                strip = jnp.concatenate([lower_ref[b, LOWER.index((i, j))] for j in range(i)], axis=1)
                total = total + dot_exact(strip, jnp.concatenate(parts[:i], axis=0))
            forward.append(dot_exact(pivot_ref[b, i] if i < 3 else last_ref[b], total))
        for i in range(4):
            total = forward[i]
            if i < 3:
                strip = jnp.concatenate([lower_ref[b, LOWER.index((j, i))] for j in range(i + 1, 4)], axis=0)
                total = total + dot_tn_exact(strip, jnp.concatenate(forward[i + 1 :], axis=0))
            steps[b * BLK + i * TILE : b * BLK + (i + 1) * TILE, :] = total
        value = steps[block, :]
        coef_ref[block, :] = value[:, :SHARE]
        high = value.astype(BF16)
        left = value - high.astype(F32)
        middle = left.astype(BF16)
        low = (left - middle.astype(F32)).astype(BF16)
        terms = lax.dot_general(
            ft_ref[block, :],
            jnp.concatenate([high, middle, low], axis=1),
            (((0,), (0,)), ((), ())),
            preferred_element_type=F32,
        )
        fit = fit + ((terms[:, 2 * TILE :] + terms[:, TILE : 2 * TILE]) + terms[:, :TILE])
    local = (labels_ref[...] - feat_ref[0] * SHARE).astype(F32)
    upright = jnp.broadcast_to(local, (TILE, ROWS)).T
    classes = lax.broadcasted_iota(jnp.int32, (ROWS, TILE), 1).astype(F32)
    targets = jnp.where(upright == classes, 1.0, 0.0)
    res_ref[...] = (targets - fit / CLS)[:, :SHARE]


def solve(feat, pivots, last, lower, own, other, rest, features, labels):
    return pl.pallas_call(
        solve_kernel,
        out_shape=(
            jax.ShapeDtypeStruct((BLOCKS * BLK, SHARE), F32),
            jax.ShapeDtypeStruct((ROWS, SHARE), F32),
        ),
        in_specs=[pl.BlockSpec(memory_space=pltpu.SMEM)] + full_specs(8),
        out_specs=(pl.BlockSpec(memory_space=VMEM), pl.BlockSpec(memory_space=VMEM)),
        scratch_shapes=[VMEM((BLOCKS * BLK, TILE), F32)],
        compiler_params=pltpu.CompilerParams(vmem_limit_bytes=VMEM_LIMIT),
        name="solve",
    )(feat, pivots, last, lower, own, other, rest, features, labels)


def gather_by_exchange(value, axis, size):
    copies = jnp.broadcast_to(value[None], (size,) + value.shape)
    return lax.all_to_all(copies, axis, 0, 0, tiled=True)


def swap_cores(value):
    return lax.ppermute(value, "c", [(0, 1), (1, 0)])


def per_device(images, labels, filters, biases):
    core = lax.axis_index("c")
    feat = (lax.axis_index("x") * 2 + core).reshape(1)
    core1 = core.reshape(1)
    panel = local_features(images, filters.reshape(LOCAL, 108), biases)
    own = lax.all_gather(panel, "x", axis=0)
    other = swap_cores(own)
    pair = jnp.where(core == 0, jnp.stack([own, other]), jnp.stack([other, own]))
    features = pair.reshape(2, 4, BLOCKS, 64, ROWS).transpose(2, 1, 0, 3, 4).reshape(BLOCKS * BLK, ROWS)

    pieces = local_products(feat, features, labels.reshape(1, ROWS))
    pieces = lax.all_to_all(pieces.reshape(4, 16 * 48, TILE), "y", 0, 0, tiled=True)
    pieces = jnp.sum(pieces, axis=0).reshape(16, 48, TILE)
    pieces = jnp.sum(lax.all_to_all(pieces, "z", 0, 0, tiled=True), axis=0)
    column = gather_by_exchange(pieces, "z", 16)

    rest = lax.all_gather(column[:, 16:], "y", axis=0).reshape(64, 32, TILE)
    diag_own = gather_by_exchange(column[:, :8], ("y", "x"), 16).reshape(DIAG_SLOTS, 4, TILE, TILE)
    diag_other = swap_cores(diag_own)
    crossing, diag_own = lax.optimization_barrier((column[:, 8:24], diag_own))
    cross_own = gather_by_exchange(crossing, ("y", "x"), 16)

    pivots, lower, last = factor(core1, diag_own, diag_other)
    last, cross_own, rest = lax.optimization_barrier((last, cross_own, rest))
    cross_own = cross_own.reshape(4, 4, 16, 16, TILE)
    cross_other = swap_cores(cross_own)
    last = last_pivots(last)
    return solve(feat, pivots, last, lower, cross_own, cross_other, rest, features, labels.reshape(1, ROWS))


def solution(mesh):
    split = Mesh(mesh.devices.reshape(4, 16, 4, 2), ("y", "z", "x", "c"))
    samp, feat = ("y", "z"), ("x", "c")
    return jax.shard_map(
        per_device,
        mesh=split,
        in_specs=(P(samp, None), P(samp), P(None, feat, None), P(None, feat)),
        out_specs=(P(None, feat), P(samp, feat)),
        check_vma=False,
    )
```

```python
import numpy as np
import jax
import jax.numpy as jnp
from jax import lax
from jax.experimental import pallas as pl
from jax.experimental.pallas import tpu as pltpu
from jax.sharding import Mesh, PartitionSpec as P

CLS = 1000
BLOCKS = 3
BLK = 512
SAMPLES = 32768
ROWS = 512
SHARE = 125
TILE = 128
LOCAL = 48
F32 = jnp.float32
BF16 = jnp.bfloat16
VMEM = pltpu.VMEM

DIAG = [(b, i, j) for b in range(BLOCKS) for i in range(4) for j in range(i + 1)]
CROSS = [(b, a, i, j) for b in range(BLOCKS) for a in range(b) for i in range(4) for j in range(4)]
DIAG_SLOTS, CROSS_SLOTS = 4, 6
LOWER = [(i, j) for i in range(4) for j in range(i)]
PANEL = 32


def tile_tables():
    table = np.zeros((8, 2 * (DIAG_SLOTS + CROSS_SLOTS)), np.int32)
    for feat in range(8):
        pairs = []
        for slot in range(DIAG_SLOTS):
            b, i, j = DIAG[min(feat * DIAG_SLOTS + slot, len(DIAG) - 1)]
            pairs.append((b * 4 + i, b * 4 + j))
        for slot in range(CROSS_SLOTS):
            b, a, i, j = CROSS[feat * CROSS_SLOTS + slot]
            pairs.append((b * 4 + i, a * 4 + j))
        table[feat] = np.array(pairs, np.int32).reshape(-1)
    return table


def tap_places():
    places = np.zeros((108, 768), np.float32)
    for c in range(3):
        for a in range(6):
            for b in range(6):
                places[c * 36 + a * 6 + b, c * 256 + a * 32 + b] = 1.0
    return places


def full_specs(count):
    return [pl.BlockSpec(memory_space=VMEM)] * count


def dot_nt(left, right):
    return lax.dot_general(left, right, (((1,), (1,)), ((), ())), preferred_element_type=F32)


def exact(left, right, over):
    return lax.dot_general(
        left, right, (over, ((), ())), precision=lax.Precision.HIGHEST, preferred_element_type=F32
    )


def dot_exact(left, right):
    return exact(left, right, ((1,), (0,)))


def dot_nt_exact(left, right):
    return exact(left, right, ((1,), (1,)))


def dot_tn_exact(left, right):
    return exact(left, right, ((0,), (0,)))


def conv_kernel(x_ref, w_ref, place_ref, bias_ref, o_ref, taps, acc, mixed):
    base = lax.dot_general(
        w_ref[...], place_ref[...], (((1,), (0,)), ((), ())), preferred_element_type=F32
    )
    for p in range(2):
        for q in range(14):
            shift = 64 * p + 2 * q
            moved = base if shift == 0 else pltpu.roll(base, shift, 1)
            row = (p * 14 + q) * LOCAL
            taps[row : row + LOCAL, :] = moved.astype(BF16)
    acc[...] = jnp.zeros_like(acc)
    square = (16, 16)
    unit = lax.broadcasted_iota(jnp.int32, square, 0) == lax.broadcasted_iota(jnp.int32, square, 1)
    spread = [jnp.broadcast_to(bias_ref[b : b + 1, :], square) for b in range(BLOCKS)]
    upright = [jnp.sum(jnp.where(unit, rows, 0.0), axis=1, keepdims=True) for rows in spread]
    bias = jnp.broadcast_to(jnp.concatenate(upright, axis=0), (LOCAL, ROWS))

    def step(t, carry):
        chunks = []
        for c in range(3):
            start = pl.multiple_of(c * 1024 + t * 128, 128)
            chunks.append(x_ref[:, pl.ds(start, 256)])
        pixels = jnp.concatenate(chunks, axis=1)
        for p in range(2):
            top = lax.select(2 * t + p >= 7, 2, 0)
            response = dot_nt(taps[p * 14 * LOCAL : (p + 1) * 14 * LOCAL, :], pixels)
            for j in range(2):
                total = None
                for q in range(7 * j, 7 * j + 7):
                    part = jnp.maximum(response[q * LOCAL : (q + 1) * LOCAL] + bias, 0.0)
                    total = part if total is None else total + part
                acc[top + j] += total
        return carry

    lax.fori_loop(0, 7, step, 0, unroll=True)
    for quadrant in range(4):
        for block in range(ROWS // TILE):
            lanes = slice(block * TILE, (block + 1) * TILE)
            mixed[block, pl.ds(quadrant, LOCAL, stride=4), :] = acc[quadrant, :, lanes] / 49.0
    for block in range(ROWS // TILE):
        o_ref[:, block * TILE : (block + 1) * TILE] = mixed[block].astype(BF16)


def local_features(images, weights, offsets):
    return pl.pallas_call(
        conv_kernel,
        out_shape=jax.ShapeDtypeStruct((4 * LOCAL, ROWS), BF16),
        in_specs=full_specs(4),
        out_specs=pl.BlockSpec(memory_space=VMEM),
        scratch_shapes=[
            VMEM((28 * LOCAL, 768), BF16),
            VMEM((4, LOCAL, ROWS), F32),
            VMEM((ROWS // TILE, 4 * LOCAL, TILE), F32),
        ],
        compiler_params=pltpu.CompilerParams(vmem_limit_bytes=24 << 20),
        name="features",
    )(images, weights, jnp.asarray(tap_places(), BF16), offsets)


def products_kernel(feat_ref, table_ref, ft_ref, labels_ref, o_ref):
    feat = feat_ref[0]

    def tile(slot):
        left = pl.multiple_of(table_ref[feat, 2 * slot] * TILE, TILE)
        right = pl.multiple_of(table_ref[feat, 2 * slot + 1] * TILE, TILE)
        return dot_nt(ft_ref[pl.ds(left, TILE), :], ft_ref[pl.ds(right, TILE), :]).reshape(16, 8, TILE)

    for slot in range(DIAG_SLOTS):
        o_ref[16 * slot : 16 * slot + 16, 0:8, :] = tile(slot)
    for slot in range(8):
        unit, place = slot // 4, slot % 4
        value = tile(DIAG_SLOTS + slot) if slot < CROSS_SLOTS else jnp.zeros((16, 8, TILE), F32)
        o_ref[16 * place : 16 * place + 16, 8 + 8 * unit : 16 + 8 * unit, :] = value
    local_class = lax.broadcasted_iota(jnp.int32, (TILE, ROWS), 0)
    hit = (labels_ref[...] == local_class + feat * SHARE) & (local_class < SHARE)
    targets = jnp.where(hit, 1.0, 0.0).astype(BF16)
    for part in range(4):
        rows = slice(part * 384, (part + 1) * 384)
        o_ref[16 * part : 16 * part + 16, 24:48, :] = dot_nt(ft_ref[rows, :], targets).reshape(16, 24, TILE)


def local_products(feat, features, labels):
    return pl.pallas_call(
        products_kernel,
        out_shape=jax.ShapeDtypeStruct((64, 48, TILE), F32),
        in_specs=[pl.BlockSpec(memory_space=pltpu.SMEM)] * 2 + full_specs(2),
        out_specs=pl.BlockSpec(memory_space=VMEM),
        compiler_params=pltpu.CompilerParams(vmem_limit_bytes=16 << 20),
        name="products",
    )(feat, jnp.asarray(tile_tables()), features, labels)


def along_lanes(value, j):
    return jnp.broadcast_to(value[:, j : j + 1], (8, TILE))


def along_rows(value, j):
    return jnp.broadcast_to(value[j : j + 1, :], (8, TILE))


def add_up(terms):
    while len(terms) > 1:
        paired = [terms[i] + terms[i + 1] for i in range(0, len(terms) - 1, 2)]
        terms = paired + ([terms[-1]] if len(terms) % 2 else [])
    return terms[0]


def small_inverses(columns, sub):
    count = len(columns)
    for r in range(8):
        here = sub == r
        rows = [[along_rows(columns[m][j], r) for j in range(8)] for m in range(count)]
        reciprocals = [1.0 / rows[m][r] for m in range(count)]
        following = [[None] * 8 for _ in range(count)]
        for j in range(8):
            for m in range(count):
                pivot = columns[m][r]
                if j == r:
                    following[m][j] = jnp.where(here, reciprocals[m], -pivot * reciprocals[m])
                else:
                    scaled = rows[m][j] * reciprocals[m]
                    following[m][j] = jnp.where(here, scaled, columns[m][j] - pivot * scaled)
        columns = following
    return columns


def invert_tiles(work):
    count = work.shape[0]
    lane = lax.broadcasted_iota(jnp.int32, (8, TILE), 1)
    sub = lax.broadcasted_iota(jnp.int32, (8, TILE), 0)
    wide_lane = lax.broadcasted_iota(jnp.int32, (TILE, TILE), 1)
    for start in range(0, TILE, PANEL):
        first, steps = start // 8, PANEL // 8
        whole = [work[m].reshape(TILE, TILE) for m in range(count)]
        panels = [[work[m, first + i] for i in range(steps)] for m in range(count)]
        for k in range(steps):
            low = start + 8 * k
            inside = (lane >= low) & (lane < low + 8)
            unit = jnp.where(lane == sub + low, 1.0, 0.0)
            inverted = small_inverses(
                [[along_lanes(panels[m][k], low + j) for j in range(8)] for m in range(count)], sub
            )
            sources = [jnp.where(inside, unit, panels[m][k]) for m in range(count)]
            solved = [
                add_up([inverted[m][j] * along_rows(sources[m], j) for j in range(8)]) for m in range(count)
            ]
            rows = [[along_rows(solved[m], j) for j in range(8)] for m in range(count)]
            following = [[None] * steps for _ in range(count)]
            for d in range(steps):
                i = (k + d) % steps
                for m in range(count):
                    if d == 0:
                        following[m][i] = solved[m]
                        continue
                    value = panels[m][i]
                    change = add_up([along_lanes(value, low + j) * rows[m][j] for j in range(8)])
                    following[m][i] = jnp.where(inside, 0.0, value) - change
            panels = following
        inside = (wide_lane >= start) & (wide_lane < start + PANEL)
        for m in range(count):
            change = dot_exact(whole[m][:, start : start + PANEL], jnp.concatenate(panels[m], axis=0))
            work[m] = (jnp.where(inside, 0.0, whole[m]) - change).reshape(16, 8, TILE)
            for i in range(steps):
                work[m, first + i] = panels[m][i]


def factor_kernel(core_ref, own_ref, other_ref, pivot_ref, lower_ref, last_ref, grid, work):
    core = core_ref[0]
    eye = jnp.where(
        lax.broadcasted_iota(jnp.int32, (TILE, TILE), 0) == lax.broadcasted_iota(jnp.int32, (TILE, TILE), 1),
        1.0,
        0.0,
    )
    traces = [jnp.zeros((1, 1), F32)] * BLOCKS
    for place, (b, i, j) in enumerate(DIAG):
        feat, slot = place // DIAG_SLOTS, place % DIAG_SLOTS
        mine, theirs = own_ref[slot, feat // 2], other_ref[slot, feat // 2]
        tile = jnp.where(core == feat % 2, mine, theirs) * (1.0 / SAMPLES)
        grid[b, i, j] = tile
        if i == j:
            diagonal = jnp.sum(tile * eye, axis=1, keepdims=True)
            traces[b] = traces[b] + jnp.sum(diagonal, axis=0, keepdims=True)
    for b in range(BLOCKS):
        ridge = 0.1 * traces[b] / BLK + 1e-05
        for i in range(4):
            grid[b, i, i] += ridge * eye

    for k in range(3):
        for b in range(BLOCKS):
            work[b] = grid[b, k, k].reshape(16, 8, TILE)
        invert_tiles(work)
        inverse = [work[b].reshape(TILE, TILE) for b in range(BLOCKS)]
        factors = {}
        for i in range(k + 1, 4):
            for b in range(BLOCKS):
                factors[b, i] = dot_exact(grid[b, i, k], inverse[b])
            for j in range(k + 1, i + 1):
                for b in range(BLOCKS):
                    grid[b, i, j] -= dot_nt_exact(factors[b, i], grid[b, j, k])
        for b in range(BLOCKS):
            pivot_ref[b, k] = inverse[b]
        for i in range(k + 1, 4):
            for b in range(BLOCKS):
                for j in range(k):
                    lower_ref[b, LOWER.index((i, j))] -= dot_exact(factors[b, i], lower_ref[b, LOWER.index((k, j))])
                lower_ref[b, LOWER.index((i, k))] = -factors[b, i]
    for b in range(BLOCKS):
        last_ref[b] = grid[b, 3, 3].reshape(16, 8, TILE)


def last_kernel(last_ref, o_ref, work):
    work[...] = last_ref[...]
    invert_tiles(work)
    o_ref[...] = work[...].reshape(BLOCKS, TILE, TILE)


def last_pivots(last):
    return pl.pallas_call(
        last_kernel,
        out_shape=jax.ShapeDtypeStruct((BLOCKS, TILE, TILE), F32),
        in_specs=full_specs(1),
        out_specs=pl.BlockSpec(memory_space=VMEM),
        scratch_shapes=[VMEM((BLOCKS, 16, 8, TILE), F32)],
        compiler_params=pltpu.CompilerParams(vmem_limit_bytes=12 << 20),
        cost_estimate=pl.CostEstimate(flops=5_000_000_000, bytes_accessed=10_000_000, transcendentals=0),
        name="last_pivots",
    )(last)


def factor(core, own, other):
    return pl.pallas_call(
        factor_kernel,
        out_shape=(
            jax.ShapeDtypeStruct((BLOCKS, 3, TILE, TILE), F32),
            jax.ShapeDtypeStruct((BLOCKS, len(LOWER), TILE, TILE), F32),
            jax.ShapeDtypeStruct((BLOCKS, 16, 8, TILE), F32),
        ),
        in_specs=[pl.BlockSpec(memory_space=pltpu.SMEM)] + full_specs(2),
        out_specs=(pl.BlockSpec(memory_space=VMEM),) * 3,
        scratch_shapes=[VMEM((BLOCKS, 4, 4, TILE, TILE), F32), VMEM((BLOCKS, 16, 8, TILE), F32)],
        compiler_params=pltpu.CompilerParams(vmem_limit_bytes=20 << 20),
        cost_estimate=pl.CostEstimate(flops=25_000_000_000, bytes_accessed=50_000_000, transcendentals=0),
        name="factor",
    )(core, own, other)


def solve_kernel(
    feat_ref, pivot_ref, last_ref, lower_ref, own_ref, other_ref, rest_ref, ft_ref, labels_ref, coef_ref, res_ref, steps
):
    core = lax.rem(feat_ref[0], 2)
    fit = jnp.zeros((ROWS, TILE), F32)
    for b in range(BLOCKS):
        block = slice(b * BLK, (b + 1) * BLK)
        parts = []
        gradient = rest_ref[b * 64 // 3 : b * 64 // 3 + 22, 8:32, :].reshape(22 * 24, TILE)
        gradient = gradient[b * BLK - b * 64 // 3 * 24 :][:BLK] * (CLS / SAMPLES)
        for i in range(4):
            total = gradient[i * TILE : (i + 1) * TILE]
            for a in range(b):
                tiles = []
                for j in range(4):
                    feat, slot = divmod(CROSS.index((b, a, i, j)), CROSS_SLOTS)
                    place = (slot % 4, feat // 2, slice(None), slice(8 * (slot // 4), 8 * (slot // 4) + 8))
                    tile = jnp.where(core == feat % 2, own_ref[place], other_ref[place])
                    tiles.append(tile.reshape(TILE, TILE))
                strip = jnp.concatenate(tiles, axis=1) * (1.0 / SAMPLES)
                total = total - dot_exact(strip, steps[a * BLK : (a + 1) * BLK, :])
            parts.append(total)
        forward = []
        for i in range(4):
            total = parts[i]
            if i:
                strip = jnp.concatenate([lower_ref[b, LOWER.index((i, j))] for j in range(i)], axis=1)
                total = total + dot_exact(strip, jnp.concatenate(parts[:i], axis=0))
            forward.append(dot_exact(pivot_ref[b, i] if i < 3 else last_ref[b], total))
        for i in range(4):
            total = forward[i]
            if i < 3:
                strip = jnp.concatenate([lower_ref[b, LOWER.index((j, i))] for j in range(i + 1, 4)], axis=0)
                total = total + dot_tn_exact(strip, jnp.concatenate(forward[i + 1 :], axis=0))
            steps[b * BLK + i * TILE : b * BLK + (i + 1) * TILE, :] = total
        value = steps[block, :]
        coef_ref[block, :] = value[:, :SHARE]
        high = value.astype(BF16)
        left = value - high.astype(F32)
        middle = left.astype(BF16)
        low = (left - middle.astype(F32)).astype(BF16)
        terms = lax.dot_general(
            ft_ref[block, :],
            jnp.concatenate([high, middle, low], axis=1),
            (((0,), (0,)), ((), ())),
            preferred_element_type=F32,
        )
        fit = fit + ((terms[:, 2 * TILE :] + terms[:, TILE : 2 * TILE]) + terms[:, :TILE])
    local = (labels_ref[...] - feat_ref[0] * SHARE).astype(F32)
    upright = jnp.broadcast_to(local, (TILE, ROWS)).T
    classes = lax.broadcasted_iota(jnp.int32, (ROWS, TILE), 1).astype(F32)
    targets = jnp.where(upright == classes, 1.0, 0.0)
    res_ref[...] = (targets - fit / CLS)[:, :SHARE]


def solve(feat, pivots, last, lower, own, other, rest, features, labels):
    return pl.pallas_call(
        solve_kernel,
        out_shape=(
            jax.ShapeDtypeStruct((BLOCKS * BLK, SHARE), F32),
            jax.ShapeDtypeStruct((ROWS, SHARE), F32),
        ),
        in_specs=[pl.BlockSpec(memory_space=pltpu.SMEM)] + full_specs(8),
        out_specs=(pl.BlockSpec(memory_space=VMEM), pl.BlockSpec(memory_space=VMEM)),
        scratch_shapes=[VMEM((BLOCKS * BLK, TILE), F32)],
        compiler_params=pltpu.CompilerParams(vmem_limit_bytes=24 << 20),
        name="solve",
    )(feat, pivots, last, lower, own, other, rest, features, labels)


def gather_by_exchange(value, axis, size):
    copies = jnp.broadcast_to(value[None], (size,) + value.shape)
    return lax.all_to_all(copies, axis, 0, 0, tiled=True)


def swap_cores(value):
    return lax.ppermute(value, "c", [(0, 1), (1, 0)])


def per_device(images, labels, filters, biases):
    core = lax.axis_index("c")
    feat = (lax.axis_index("x") * 2 + core).reshape(1)
    core1 = core.reshape(1)
    panel = local_features(images, filters.reshape(LOCAL, 108), biases)
    own = lax.all_gather(panel, "x", axis=0)
    other = swap_cores(own)
    pair = jnp.where(core == 0, jnp.stack([own, other]), jnp.stack([other, own]))
    features = pair.reshape(2, 4, BLOCKS, 64, ROWS).transpose(2, 1, 0, 3, 4).reshape(BLOCKS * BLK, ROWS)

    pieces = local_products(feat, features, labels.reshape(1, ROWS))
    pieces = lax.all_to_all(pieces.reshape(4, 16 * 48, TILE), "y", 0, 0, tiled=True)
    pieces = jnp.sum(pieces, axis=0).reshape(16, 48, TILE)
    pieces = jnp.sum(lax.all_to_all(pieces, "z", 0, 0, tiled=True), axis=0)
    column = gather_by_exchange(pieces, "z", 16)

    rest = lax.all_gather(column[:, 16:], "y", axis=0).reshape(64, 32, TILE)
    diag_own = gather_by_exchange(column[:, :8], ("y", "x"), 16).reshape(DIAG_SLOTS, 4, TILE, TILE)
    diag_other = swap_cores(diag_own)
    crossing, diag_own, rest = lax.optimization_barrier((column[:, 8:24], diag_own, rest))
    cross_own = gather_by_exchange(crossing, ("y", "x"), 16)

    pivots, lower, last = factor(core1, diag_own, diag_other)
    last, cross_own = lax.optimization_barrier((last, cross_own))
    cross_own = cross_own.reshape(4, 4, 16, 16, TILE)
    cross_other = swap_cores(cross_own)
    last = last_pivots(last)
    return solve(feat, pivots, last, lower, cross_own, cross_other, rest, features, labels.reshape(1, ROWS))


def solution(mesh):
    split = Mesh(mesh.devices.reshape(4, 16, 4, 2), ("y", "z", "x", "c"))
    samp, feat = ("y", "z"), ("x", "c")
    return jax.shard_map(
        per_device,
        mesh=split,
        in_specs=(P(samp, None), P(samp), P(None, feat, None), P(None, feat)),
        out_specs=(P(None, feat), P(samp, feat)),
        check_vma=False,
    )
```

```python
import numpy as np
import jax
import jax.numpy as jnp
from jax import lax
from jax.experimental import pallas as pl
from jax.experimental.pallas import tpu as pltpu
from jax.sharding import Mesh, PartitionSpec as P

CLS = 1000
BLOCKS = 3
BLK = 512
SAMPLES = 32768
ROWS = 512
SHARE = 125
TILE = 128
LOCAL = 48
F32 = jnp.float32
BF16 = jnp.bfloat16
VMEM = pltpu.VMEM

DIAG = [(b, i, j) for b in range(BLOCKS) for i in range(4) for j in range(i + 1)]
CROSS = [(b, a, i, j) for b in range(BLOCKS) for a in range(b) for i in range(4) for j in range(4)]
DIAG_SLOTS, CROSS_SLOTS = 4, 6
LOWER = [(i, j) for i in range(4) for j in range(i)]
PANEL = 32


def tile_tables():
    table = np.zeros((8, 2 * (DIAG_SLOTS + CROSS_SLOTS)), np.int32)
    for feat in range(8):
        pairs = []
        for slot in range(DIAG_SLOTS):
            b, i, j = DIAG[min(feat * DIAG_SLOTS + slot, len(DIAG) - 1)]
            pairs.append((b * 4 + i, b * 4 + j))
        for slot in range(CROSS_SLOTS):
            b, a, i, j = CROSS[feat * CROSS_SLOTS + slot]
            pairs.append((b * 4 + i, a * 4 + j))
        table[feat] = np.array(pairs, np.int32).reshape(-1)
    return table


def tap_places():
    places = np.zeros((108, 768), np.float32)
    for c in range(3):
        for a in range(6):
            for b in range(6):
                places[c * 36 + a * 6 + b, c * 256 + a * 32 + b] = 1.0
    return places


def full_specs(count):
    return [pl.BlockSpec(memory_space=VMEM)] * count


def dot_nt(left, right):
    return lax.dot_general(left, right, (((1,), (1,)), ((), ())), preferred_element_type=F32)


def exact(left, right, over):
    return lax.dot_general(
        left, right, (over, ((), ())), precision=lax.Precision.HIGHEST, preferred_element_type=F32
    )


def dot_exact(left, right):
    return exact(left, right, ((1,), (0,)))


def dot_nt_exact(left, right):
    return exact(left, right, ((1,), (1,)))


def dot_tn_exact(left, right):
    return exact(left, right, ((0,), (0,)))


def conv_kernel(x_ref, w_ref, place_ref, bias_ref, o_ref, taps, acc, mixed):
    base = lax.dot_general(
        w_ref[...], place_ref[...], (((1,), (0,)), ((), ())), preferred_element_type=F32
    )
    for p in range(2):
        for q in range(14):
            shift = 64 * p + 2 * q
            moved = base if shift == 0 else pltpu.roll(base, shift, 1)
            row = (p * 14 + q) * LOCAL
            taps[row : row + LOCAL, :] = moved.astype(BF16)
    acc[...] = jnp.zeros_like(acc)
    square = (16, 16)
    unit = lax.broadcasted_iota(jnp.int32, square, 0) == lax.broadcasted_iota(jnp.int32, square, 1)
    spread = [jnp.broadcast_to(bias_ref[b : b + 1, :], square) for b in range(BLOCKS)]
    upright = [jnp.sum(jnp.where(unit, rows, 0.0), axis=1, keepdims=True) for rows in spread]
    bias = jnp.broadcast_to(jnp.concatenate(upright, axis=0), (LOCAL, ROWS))

    def step(t, carry):
        chunks = []
        for c in range(3):
            start = pl.multiple_of(c * 1024 + t * 128, 128)
            chunks.append(x_ref[:, pl.ds(start, 256)])
        pixels = jnp.concatenate(chunks, axis=1)
        for p in range(2):
            top = lax.select(2 * t + p >= 7, 2, 0)
            response = dot_nt(taps[p * 14 * LOCAL : (p + 1) * 14 * LOCAL, :], pixels)
            for j in range(2):
                total = None
                for q in range(7 * j, 7 * j + 7):
                    part = jnp.maximum(response[q * LOCAL : (q + 1) * LOCAL] + bias, 0.0)
                    total = part if total is None else total + part
                acc[top + j] += total
        return carry

    lax.fori_loop(0, 7, step, 0, unroll=True)
    for quadrant in range(4):
        for block in range(ROWS // TILE):
            lanes = slice(block * TILE, (block + 1) * TILE)
            mixed[block, pl.ds(quadrant, LOCAL, stride=4), :] = acc[quadrant, :, lanes] / 49.0
    for block in range(ROWS // TILE):
        o_ref[:, block * TILE : (block + 1) * TILE] = mixed[block].astype(BF16)


def local_features(images, weights, offsets):
    return pl.pallas_call(
        conv_kernel,
        out_shape=jax.ShapeDtypeStruct((4 * LOCAL, ROWS), BF16),
        in_specs=full_specs(4),
        out_specs=pl.BlockSpec(memory_space=VMEM),
        scratch_shapes=[
            VMEM((28 * LOCAL, 768), BF16),
            VMEM((4, LOCAL, ROWS), F32),
            VMEM((ROWS // TILE, 4 * LOCAL, TILE), F32),
        ],
        compiler_params=pltpu.CompilerParams(vmem_limit_bytes=24 << 20),
        name="features",
    )(images, weights, jnp.asarray(tap_places(), BF16), offsets)


def products_kernel(feat_ref, table_ref, ft_ref, labels_ref, o_ref):
    feat = feat_ref[0]

    def tile(slot):
        left = pl.multiple_of(table_ref[feat, 2 * slot] * TILE, TILE)
        right = pl.multiple_of(table_ref[feat, 2 * slot + 1] * TILE, TILE)
        return dot_nt(ft_ref[pl.ds(left, TILE), :], ft_ref[pl.ds(right, TILE), :]).reshape(16, 8, TILE)

    for slot in range(DIAG_SLOTS):
        o_ref[16 * slot : 16 * slot + 16, 0:8, :] = tile(slot)
    for slot in range(8):
        unit, place = slot // 4, slot % 4
        value = tile(DIAG_SLOTS + slot) if slot < CROSS_SLOTS else jnp.zeros((16, 8, TILE), F32)
        o_ref[16 * place : 16 * place + 16, 8 + 8 * unit : 16 + 8 * unit, :] = value
    local_class = lax.broadcasted_iota(jnp.int32, (TILE, ROWS), 0)
    hit = (labels_ref[...] == local_class + feat * SHARE) & (local_class < SHARE)
    targets = jnp.where(hit, 1.0, 0.0).astype(BF16)
    for part in range(4):
        rows = slice(part * 384, (part + 1) * 384)
        o_ref[16 * part : 16 * part + 16, 24:48, :] = dot_nt(ft_ref[rows, :], targets).reshape(16, 24, TILE)


def local_products(feat, features, labels):
    return pl.pallas_call(
        products_kernel,
        out_shape=jax.ShapeDtypeStruct((64, 48, TILE), F32),
        in_specs=[pl.BlockSpec(memory_space=pltpu.SMEM)] * 2 + full_specs(2),
        out_specs=pl.BlockSpec(memory_space=VMEM),
        compiler_params=pltpu.CompilerParams(vmem_limit_bytes=16 << 20),
        name="products",
    )(feat, jnp.asarray(tile_tables()), features, labels)


def along_lanes(value, j):
    return jnp.broadcast_to(value[:, j : j + 1], (8, TILE))


def along_rows(value, j):
    return jnp.broadcast_to(value[j : j + 1, :], (8, TILE))


def add_up(terms):
    while len(terms) > 1:
        paired = [terms[i] + terms[i + 1] for i in range(0, len(terms) - 1, 2)]
        terms = paired + ([terms[-1]] if len(terms) % 2 else [])
    return terms[0]


def small_inverses(columns, sub):
    count = len(columns)
    for r in range(8):
        here = sub == r
        rows = [[along_rows(columns[m][j], r) for j in range(8)] for m in range(count)]
        reciprocals = [1.0 / rows[m][r] for m in range(count)]
        following = [[None] * 8 for _ in range(count)]
        for j in range(8):
            for m in range(count):
                pivot = columns[m][r]
                if j == r:
                    following[m][j] = jnp.where(here, reciprocals[m], -pivot * reciprocals[m])
                else:
                    scaled = rows[m][j] * reciprocals[m]
                    following[m][j] = jnp.where(here, scaled, columns[m][j] - pivot * scaled)
        columns = following
    return columns


def invert_tiles(work):
    count = work.shape[0]
    lane = lax.broadcasted_iota(jnp.int32, (8, TILE), 1)
    sub = lax.broadcasted_iota(jnp.int32, (8, TILE), 0)
    wide_lane = lax.broadcasted_iota(jnp.int32, (TILE, TILE), 1)
    for start in range(0, TILE, PANEL):
        first, steps = start // 8, PANEL // 8
        whole = [work[m].reshape(TILE, TILE) for m in range(count)]
        panels = [[work[m, first + i] for i in range(steps)] for m in range(count)]
        for k in range(steps):
            low = start + 8 * k
            inside = (lane >= low) & (lane < low + 8)
            unit = jnp.where(lane == sub + low, 1.0, 0.0)
            inverted = small_inverses(
                [[along_lanes(panels[m][k], low + j) for j in range(8)] for m in range(count)], sub
            )
            sources = [jnp.where(inside, unit, panels[m][k]) for m in range(count)]
            solved = [
                add_up([inverted[m][j] * along_rows(sources[m], j) for j in range(8)]) for m in range(count)
            ]
            rows = [[along_rows(solved[m], j) for j in range(8)] for m in range(count)]
            following = [[None] * steps for _ in range(count)]
            for d in range(steps):
                i = (k + d) % steps
                for m in range(count):
                    if d == 0:
                        following[m][i] = solved[m]
                        continue
                    value = panels[m][i]
                    change = add_up([along_lanes(value, low + j) * rows[m][j] for j in range(8)])
                    following[m][i] = jnp.where(inside, 0.0, value) - change
            panels = following
        inside = (wide_lane >= start) & (wide_lane < start + PANEL)
        for m in range(count):
            change = dot_exact(whole[m][:, start : start + PANEL], jnp.concatenate(panels[m], axis=0))
            work[m] = (jnp.where(inside, 0.0, whole[m]) - change).reshape(16, 8, TILE)
            for i in range(steps):
                work[m, first + i] = panels[m][i]


def factor_kernel(core_ref, own_ref, other_ref, pivot_ref, lower_ref, last_ref, grid, work):
    core = core_ref[0]
    eye = jnp.where(
        lax.broadcasted_iota(jnp.int32, (TILE, TILE), 0) == lax.broadcasted_iota(jnp.int32, (TILE, TILE), 1),
        1.0,
        0.0,
    )
    traces = [jnp.zeros((1, 1), F32)] * BLOCKS
    for place, (b, i, j) in enumerate(DIAG):
        feat, slot = place // DIAG_SLOTS, place % DIAG_SLOTS
        mine, theirs = own_ref[slot, feat // 2], other_ref[slot, feat // 2]
        tile = jnp.where(core == feat % 2, mine, theirs) * (1.0 / SAMPLES)
        grid[b, i, j] = tile
        if i == j:
            diagonal = jnp.sum(tile * eye, axis=1, keepdims=True)
            traces[b] = traces[b] + jnp.sum(diagonal, axis=0, keepdims=True)
    for b in range(BLOCKS):
        ridge = 0.1 * traces[b] / BLK + 1e-05
        for i in range(4):
            grid[b, i, i] += ridge * eye

    for k in range(3):
        for b in range(BLOCKS):
            work[b] = grid[b, k, k].reshape(16, 8, TILE)
        invert_tiles(work)
        inverse = [work[b].reshape(TILE, TILE) for b in range(BLOCKS)]
        factors = {}
        for i in range(k + 1, 4):
            for b in range(BLOCKS):
                factors[b, i] = dot_exact(grid[b, i, k], inverse[b])
            for j in range(k + 1, i + 1):
                for b in range(BLOCKS):
                    grid[b, i, j] -= dot_nt_exact(factors[b, i], grid[b, j, k])
        for b in range(BLOCKS):
            pivot_ref[b, k] = inverse[b]
        for i in range(k + 1, 4):
            for b in range(BLOCKS):
                for j in range(k):
                    lower_ref[b, LOWER.index((i, j))] -= dot_exact(factors[b, i], lower_ref[b, LOWER.index((k, j))])
                lower_ref[b, LOWER.index((i, k))] = -factors[b, i]
    for b in range(BLOCKS):
        last_ref[b] = grid[b, 3, 3].reshape(16, 8, TILE)


def last_kernel(last_ref, o_ref, work):
    work[...] = last_ref[...]
    invert_tiles(work)
    o_ref[...] = work[...].reshape(BLOCKS, TILE, TILE)


def last_pivots(last):
    return pl.pallas_call(
        last_kernel,
        out_shape=jax.ShapeDtypeStruct((BLOCKS, TILE, TILE), F32),
        in_specs=full_specs(1),
        out_specs=pl.BlockSpec(memory_space=VMEM),
        scratch_shapes=[VMEM((BLOCKS, 16, 8, TILE), F32)],
        compiler_params=pltpu.CompilerParams(vmem_limit_bytes=12 << 20),
        cost_estimate=pl.CostEstimate(flops=5_000_000_000, bytes_accessed=10_000_000, transcendentals=0),
        name="last_pivots",
    )(last)


def factor(core, own, other):
    return pl.pallas_call(
        factor_kernel,
        out_shape=(
            jax.ShapeDtypeStruct((BLOCKS, 3, TILE, TILE), F32),
            jax.ShapeDtypeStruct((BLOCKS, len(LOWER), TILE, TILE), F32),
            jax.ShapeDtypeStruct((BLOCKS, 16, 8, TILE), F32),
        ),
        in_specs=[pl.BlockSpec(memory_space=pltpu.SMEM)] + full_specs(2),
        out_specs=(pl.BlockSpec(memory_space=VMEM),) * 3,
        scratch_shapes=[VMEM((BLOCKS, 4, 4, TILE, TILE), F32), VMEM((BLOCKS, 16, 8, TILE), F32)],
        compiler_params=pltpu.CompilerParams(vmem_limit_bytes=20 << 20),
        cost_estimate=pl.CostEstimate(flops=25_000_000_000, bytes_accessed=50_000_000, transcendentals=0),
        name="factor",
    )(core, own, other)


def solve_kernel(
    feat_ref, pivot_ref, last_ref, lower_ref, own_ref, other_ref, s0, s1, s2, s3, ft_ref, labels_ref, coef_ref, res_ref, steps
):
    core = lax.rem(feat_ref[0], 2)
    for d, share_ref in enumerate((s0, s1, s2, s3)):
        origin = lax.rem(feat_ref[1] + 4 - d, 4)
        steps[pl.ds(pl.multiple_of(origin * 384, 128), 384), :] = share_ref[...].reshape(384, TILE)
    fit = jnp.zeros((ROWS, TILE), F32)
    for b in range(BLOCKS):
        block = slice(b * BLK, (b + 1) * BLK)
        parts = []
        gradient = steps[block, :] * (CLS / SAMPLES)
        for i in range(4):
            total = gradient[i * TILE : (i + 1) * TILE]
            for a in range(b):
                tiles = []
                for j in range(4):
                    feat, slot = divmod(CROSS.index((b, a, i, j)), CROSS_SLOTS)
                    place = (slot % 4, feat // 2, slice(None), slice(8 * (slot // 4), 8 * (slot // 4) + 8))
                    tile = jnp.where(core == feat % 2, own_ref[place], other_ref[place])
                    tiles.append(tile.reshape(TILE, TILE))
                strip = jnp.concatenate(tiles, axis=1) * (1.0 / SAMPLES)
                total = total - dot_exact(strip, steps[a * BLK : (a + 1) * BLK, :])
            parts.append(total)
        forward = []
        for i in range(4):
            total = parts[i]
            if i:
                strip = jnp.concatenate([lower_ref[b, LOWER.index((i, j))] for j in range(i)], axis=1)
                total = total + dot_exact(strip, jnp.concatenate(parts[:i], axis=0))
            forward.append(dot_exact(pivot_ref[b, i] if i < 3 else last_ref[b], total))
        for i in range(4):
            total = forward[i]
            if i < 3:
                strip = jnp.concatenate([lower_ref[b, LOWER.index((j, i))] for j in range(i + 1, 4)], axis=0)
                total = total + dot_tn_exact(strip, jnp.concatenate(forward[i + 1 :], axis=0))
            steps[b * BLK + i * TILE : b * BLK + (i + 1) * TILE, :] = total
        value = steps[block, :]
        coef_ref[block, :] = value[:, :SHARE]
        high = value.astype(BF16)
        left = value - high.astype(F32)
        middle = left.astype(BF16)
        low = (left - middle.astype(F32)).astype(BF16)
        terms = lax.dot_general(
            ft_ref[block, :],
            jnp.concatenate([high, middle, low], axis=1),
            (((0,), (0,)), ((), ())),
            preferred_element_type=F32,
        )
        fit = fit + ((terms[:, 2 * TILE :] + terms[:, TILE : 2 * TILE]) + terms[:, :TILE])
    local = (labels_ref[...] - feat_ref[0] * SHARE).astype(F32)
    upright = jnp.broadcast_to(local, (TILE, ROWS)).T
    classes = lax.broadcasted_iota(jnp.int32, (ROWS, TILE), 1).astype(F32)
    targets = jnp.where(upright == classes, 1.0, 0.0)
    res_ref[...] = (targets - fit / CLS)[:, :SHARE]


def solve(feat, pivots, last, lower, own, other, shares, features, labels):
    return pl.pallas_call(
        solve_kernel,
        out_shape=(
            jax.ShapeDtypeStruct((BLOCKS * BLK, SHARE), F32),
            jax.ShapeDtypeStruct((ROWS, SHARE), F32),
        ),
        in_specs=[pl.BlockSpec(memory_space=pltpu.SMEM)] + full_specs(11),
        out_specs=(pl.BlockSpec(memory_space=VMEM), pl.BlockSpec(memory_space=VMEM)),
        scratch_shapes=[VMEM((BLOCKS * BLK, TILE), F32)],
        compiler_params=pltpu.CompilerParams(vmem_limit_bytes=24 << 20),
        name="solve",
    )(feat, pivots, last, lower, own, other, *shares, features, labels)


def gather_by_exchange(value, axis, size):
    copies = jnp.broadcast_to(value[None], (size,) + value.shape)
    return lax.all_to_all(copies, axis, 0, 0, tiled=True)


def swap_cores(value):
    return lax.ppermute(value, "c", [(0, 1), (1, 0)])


def per_device(images, labels, filters, biases):
    core = lax.axis_index("c")
    feat = (lax.axis_index("x") * 2 + core).reshape(1)
    core1 = core.reshape(1)
    panel = local_features(images, filters.reshape(LOCAL, 108), biases)
    own = lax.all_gather(panel, "x", axis=0)
    other = swap_cores(own)
    pair = jnp.where(core == 0, jnp.stack([own, other]), jnp.stack([other, own]))
    features = pair.reshape(2, 4, BLOCKS, 64, ROWS).transpose(2, 1, 0, 3, 4).reshape(BLOCKS * BLK, ROWS)

    pieces = local_products(feat, features, labels.reshape(1, ROWS))
    pieces = lax.all_to_all(pieces.reshape(4, 16 * 48, TILE), "y", 0, 0, tiled=True)
    pieces = jnp.sum(pieces, axis=0).reshape(16, 48, TILE)
    pieces = jnp.sum(lax.all_to_all(pieces, "z", 0, 0, tiled=True), axis=0)
    column = gather_by_exchange(pieces, "z", 16)

    share = column[:, 24:]
    steps = [share] + [lax.ppermute(share, "y", [(i, (i + d) % 4) for i in range(4)]) for d in (1, 2, 3)]
    diag_own = gather_by_exchange(column[:, :8], ("y", "x"), 16).reshape(DIAG_SLOTS, 4, TILE, TILE)
    diag_other = swap_cores(diag_own)
    crossing, diag_own = lax.optimization_barrier((column[:, 8:24], diag_own))
    cross_own = gather_by_exchange(crossing, ("y", "x"), 16)

    pivots, lower, last = factor(core1, diag_own, diag_other)
    last, cross_own = lax.optimization_barrier((last, cross_own))
    cross_own = cross_own.reshape(4, 4, 16, 16, TILE)
    cross_other = swap_cores(cross_own)
    last = last_pivots(last)
    return solve(jnp.stack([feat[0], lax.axis_index("y")]), pivots, last, lower, cross_own, cross_other, steps, features, labels.reshape(1, ROWS))


def solution(mesh):
    split = Mesh(mesh.devices.reshape(4, 16, 4, 2), ("y", "z", "x", "c"))
    samp, feat = ("y", "z"), ("x", "c")
    return jax.shard_map(
        per_device,
        mesh=split,
        in_specs=(P(samp, None), P(samp), P(None, feat, None), P(None, feat)),
        out_specs=(P(None, feat), P(samp, feat)),
        check_vma=False,
    )
```

```python
import numpy as np
import jax
import jax.numpy as jnp
from jax import lax
from jax.experimental import pallas as pl
from jax.experimental.pallas import tpu as pltpu
from jax.sharding import Mesh, PartitionSpec as P

CLS = 1000
BLOCKS = 3
BLK = 512
SAMPLES = 32768
ROWS = 512
SHARE = 125
TILE = 128
LOCAL = 48
F32 = jnp.float32
BF16 = jnp.bfloat16
VMEM = pltpu.VMEM

DIAG = [(b, i, j) for b in range(BLOCKS) for i in range(4) for j in range(i + 1)]
CROSS = [(b, a, i, j) for b in range(BLOCKS) for a in range(b) for i in range(4) for j in range(4)]
DIAG_SLOTS, CROSS_SLOTS = 4, 6
LOWER = [(i, j) for i in range(4) for j in range(i)]
PANEL = 32


def tile_tables():
    table = np.zeros((8, 2 * (DIAG_SLOTS + CROSS_SLOTS)), np.int32)
    for feat in range(8):
        pairs = []
        for slot in range(DIAG_SLOTS):
            b, i, j = DIAG[min(feat * DIAG_SLOTS + slot, len(DIAG) - 1)]
            pairs.append((b * 4 + i, b * 4 + j))
        for slot in range(CROSS_SLOTS):
            b, a, i, j = CROSS[feat * CROSS_SLOTS + slot]
            pairs.append((b * 4 + i, a * 4 + j))
        table[feat] = np.array(pairs, np.int32).reshape(-1)
    return table


def tap_places():
    places = np.zeros((108, 768), np.float32)
    for c in range(3):
        for a in range(6):
            for b in range(6):
                places[c * 36 + a * 6 + b, c * 256 + a * 32 + b] = 1.0
    return places


def full_specs(count):
    return [pl.BlockSpec(memory_space=VMEM)] * count


def dot_nt(left, right):
    return lax.dot_general(left, right, (((1,), (1,)), ((), ())), preferred_element_type=F32)


def exact(left, right, over):
    return lax.dot_general(
        left, right, (over, ((), ())), precision=lax.Precision.HIGHEST, preferred_element_type=F32
    )


def dot_exact(left, right):
    return exact(left, right, ((1,), (0,)))


def dot_nt_exact(left, right):
    return exact(left, right, ((1,), (1,)))


def dot_tn_exact(left, right):
    return exact(left, right, ((0,), (0,)))


def conv_kernel(x_ref, w_ref, place_ref, bias_ref, o_ref, taps, acc, mixed):
    base = lax.dot_general(
        w_ref[...], place_ref[...], (((1,), (0,)), ((), ())), preferred_element_type=F32
    )
    for p in range(2):
        for q in range(14):
            shift = 64 * p + 2 * q
            moved = base if shift == 0 else pltpu.roll(base, shift, 1)
            row = (p * 14 + q) * LOCAL
            taps[row : row + LOCAL, :] = moved.astype(BF16)
    acc[...] = jnp.zeros_like(acc)
    square = (16, 16)
    unit = lax.broadcasted_iota(jnp.int32, square, 0) == lax.broadcasted_iota(jnp.int32, square, 1)
    spread = [jnp.broadcast_to(bias_ref[b : b + 1, :], square) for b in range(BLOCKS)]
    upright = [jnp.sum(jnp.where(unit, rows, 0.0), axis=1, keepdims=True) for rows in spread]
    bias = jnp.broadcast_to(jnp.concatenate(upright, axis=0), (LOCAL, ROWS))

    def step(t, carry):
        chunks = []
        for c in range(3):
            start = pl.multiple_of(c * 1024 + t * 128, 128)
            chunks.append(x_ref[:, pl.ds(start, 256)])
        pixels = jnp.concatenate(chunks, axis=1)
        for p in range(2):
            top = lax.select(2 * t + p >= 7, 2, 0)
            response = dot_nt(taps[p * 14 * LOCAL : (p + 1) * 14 * LOCAL, :], pixels)
            for j in range(2):
                total = None
                for q in range(7 * j, 7 * j + 7):
                    part = jnp.maximum(response[q * LOCAL : (q + 1) * LOCAL] + bias, 0.0)
                    total = part if total is None else total + part
                acc[top + j] += total
        return carry

    lax.fori_loop(0, 7, step, 0, unroll=True)
    for quadrant in range(4):
        for block in range(ROWS // TILE):
            lanes = slice(block * TILE, (block + 1) * TILE)
            mixed[block, pl.ds(quadrant, LOCAL, stride=4), :] = acc[quadrant, :, lanes] / 49.0
    for block in range(ROWS // TILE):
        o_ref[:, block * TILE : (block + 1) * TILE] = mixed[block].astype(BF16)


def local_features(images, weights, offsets):
    return pl.pallas_call(
        conv_kernel,
        out_shape=jax.ShapeDtypeStruct((4 * LOCAL, ROWS), BF16),
        in_specs=full_specs(4),
        out_specs=pl.BlockSpec(memory_space=VMEM),
        scratch_shapes=[
            VMEM((28 * LOCAL, 768), BF16),
            VMEM((4, LOCAL, ROWS), F32),
            VMEM((ROWS // TILE, 4 * LOCAL, TILE), F32),
        ],
        compiler_params=pltpu.CompilerParams(vmem_limit_bytes=24 << 20),
        name="features",
    )(images, weights, jnp.asarray(tap_places(), BF16), offsets)


def products_kernel(feat_ref, table_ref, ft_ref, labels_ref, o_ref):
    feat = feat_ref[0]

    def tile(slot):
        left = pl.multiple_of(table_ref[feat, 2 * slot] * TILE, TILE)
        right = pl.multiple_of(table_ref[feat, 2 * slot + 1] * TILE, TILE)
        return dot_nt(ft_ref[pl.ds(left, TILE), :], ft_ref[pl.ds(right, TILE), :]).reshape(16, 8, TILE)

    for slot in range(DIAG_SLOTS):
        o_ref[16 * slot : 16 * slot + 16, 0:8, :] = tile(slot)
    for slot in range(8):
        unit, place = slot // 4, slot % 4
        value = tile(DIAG_SLOTS + slot) if slot < CROSS_SLOTS else jnp.zeros((16, 8, TILE), F32)
        o_ref[16 * place : 16 * place + 16, 8 + 8 * unit : 16 + 8 * unit, :] = value
    local_class = lax.broadcasted_iota(jnp.int32, (TILE, ROWS), 0)
    hit = (labels_ref[...] == local_class + feat * SHARE) & (local_class < SHARE)
    targets = jnp.where(hit, 1.0, 0.0).astype(BF16)
    for part in range(4):
        rows = slice(part * 384, (part + 1) * 384)
        o_ref[16 * part : 16 * part + 16, 24:48, :] = dot_nt(ft_ref[rows, :], targets).reshape(16, 24, TILE)


def local_products(feat, features, labels):
    return pl.pallas_call(
        products_kernel,
        out_shape=jax.ShapeDtypeStruct((64, 48, TILE), F32),
        in_specs=[pl.BlockSpec(memory_space=pltpu.SMEM)] * 2 + full_specs(2),
        out_specs=pl.BlockSpec(memory_space=VMEM),
        compiler_params=pltpu.CompilerParams(vmem_limit_bytes=16 << 20),
        name="products",
    )(feat, jnp.asarray(tile_tables()), features, labels)


def along_lanes(value, j):
    return jnp.broadcast_to(value[:, j : j + 1], (8, TILE))


def along_rows(value, j):
    return jnp.broadcast_to(value[j : j + 1, :], (8, TILE))


def add_up(terms):
    while len(terms) > 1:
        paired = [terms[i] + terms[i + 1] for i in range(0, len(terms) - 1, 2)]
        terms = paired + ([terms[-1]] if len(terms) % 2 else [])
    return terms[0]


def small_inverses(columns, sub):
    count = len(columns)
    for r in range(8):
        here = sub == r
        rows = [[along_rows(columns[m][j], r) for j in range(8)] for m in range(count)]
        reciprocals = [1.0 / rows[m][r] for m in range(count)]
        following = [[None] * 8 for _ in range(count)]
        for j in range(8):
            for m in range(count):
                pivot = columns[m][r]
                if j == r:
                    following[m][j] = jnp.where(here, reciprocals[m], -pivot * reciprocals[m])
                else:
                    scaled = rows[m][j] * reciprocals[m]
                    following[m][j] = jnp.where(here, scaled, columns[m][j] - pivot * scaled)
        columns = following
    return columns


def invert_tiles(work):
    count = work.shape[0]
    lane = lax.broadcasted_iota(jnp.int32, (8, TILE), 1)
    sub = lax.broadcasted_iota(jnp.int32, (8, TILE), 0)
    wide_lane = lax.broadcasted_iota(jnp.int32, (TILE, TILE), 1)
    for start in range(0, TILE, PANEL):
        first, steps = start // 8, PANEL // 8
        whole = [work[m].reshape(TILE, TILE) for m in range(count)]
        panels = [[work[m, first + i] for i in range(steps)] for m in range(count)]
        for k in range(steps):
            low = start + 8 * k
            inside = (lane >= low) & (lane < low + 8)
            unit = jnp.where(lane == sub + low, 1.0, 0.0)
            inverted = small_inverses(
                [[along_lanes(panels[m][k], low + j) for j in range(8)] for m in range(count)], sub
            )
            sources = [jnp.where(inside, unit, panels[m][k]) for m in range(count)]
            solved = [
                add_up([inverted[m][j] * along_rows(sources[m], j) for j in range(8)]) for m in range(count)
            ]
            rows = [[along_rows(solved[m], j) for j in range(8)] for m in range(count)]
            following = [[None] * steps for _ in range(count)]
            for d in range(steps):
                i = (k + d) % steps
                for m in range(count):
                    if d == 0:
                        following[m][i] = solved[m]
                        continue
                    value = panels[m][i]
                    change = add_up([along_lanes(value, low + j) * rows[m][j] for j in range(8)])
                    following[m][i] = jnp.where(inside, 0.0, value) - change
            panels = following
        inside = (wide_lane >= start) & (wide_lane < start + PANEL)
        for m in range(count):
            change = dot_exact(whole[m][:, start : start + PANEL], jnp.concatenate(panels[m], axis=0))
            work[m] = (jnp.where(inside, 0.0, whole[m]) - change).reshape(16, 8, TILE)
            for i in range(steps):
                work[m, first + i] = panels[m][i]


def factor_kernel(core_ref, own_ref, other_ref, pivot_ref, lower_ref, last_ref, grid, work):
    core = core_ref[0]
    eye = jnp.where(
        lax.broadcasted_iota(jnp.int32, (TILE, TILE), 0) == lax.broadcasted_iota(jnp.int32, (TILE, TILE), 1),
        1.0,
        0.0,
    )
    traces = [jnp.zeros((1, 1), F32)] * BLOCKS
    for place, (b, i, j) in enumerate(DIAG):
        feat, slot = place // DIAG_SLOTS, place % DIAG_SLOTS
        mine, theirs = own_ref[slot, feat // 2], other_ref[slot, feat // 2]
        tile = jnp.where(core == feat % 2, mine, theirs) * (1.0 / SAMPLES)
        grid[b, i, j] = tile
        if i == j:
            diagonal = jnp.sum(tile * eye, axis=1, keepdims=True)
            traces[b] = traces[b] + jnp.sum(diagonal, axis=0, keepdims=True)
    for b in range(BLOCKS):
        ridge = 0.1 * traces[b] / BLK + 1e-05
        for i in range(4):
            grid[b, i, i] += ridge * eye

    for k in range(3):
        for b in range(BLOCKS):
            work[b] = grid[b, k, k].reshape(16, 8, TILE)
        invert_tiles(work)
        inverse = [work[b].reshape(TILE, TILE) for b in range(BLOCKS)]
        factors = {}
        for i in range(k + 1, 4):
            for b in range(BLOCKS):
                factors[b, i] = dot_exact(grid[b, i, k], inverse[b])
            for j in range(k + 1, i + 1):
                for b in range(BLOCKS):
                    grid[b, i, j] -= dot_nt_exact(factors[b, i], grid[b, j, k])
        for b in range(BLOCKS):
            pivot_ref[b, k] = inverse[b]
        for i in range(k + 1, 4):
            for b in range(BLOCKS):
                for j in range(k):
                    lower_ref[b, LOWER.index((i, j))] -= dot_exact(factors[b, i], lower_ref[b, LOWER.index((k, j))])
                lower_ref[b, LOWER.index((i, k))] = -factors[b, i]
    for b in range(BLOCKS):
        last_ref[b] = grid[b, 3, 3].reshape(16, 8, TILE)


def last_kernel(last_ref, o_ref, work):
    work[...] = last_ref[...]
    invert_tiles(work)
    o_ref[...] = work[...].reshape(BLOCKS, TILE, TILE)


def last_pivots(last):
    return pl.pallas_call(
        last_kernel,
        out_shape=jax.ShapeDtypeStruct((BLOCKS, TILE, TILE), F32),
        in_specs=full_specs(1),
        out_specs=pl.BlockSpec(memory_space=VMEM),
        scratch_shapes=[VMEM((BLOCKS, 16, 8, TILE), F32)],
        compiler_params=pltpu.CompilerParams(vmem_limit_bytes=12 << 20),
        cost_estimate=pl.CostEstimate(flops=5_000_000_000, bytes_accessed=10_000_000, transcendentals=0),
        name="last_pivots",
    )(last)


def factor(core, own, other):
    return pl.pallas_call(
        factor_kernel,
        out_shape=(
            jax.ShapeDtypeStruct((BLOCKS, 3, TILE, TILE), F32),
            jax.ShapeDtypeStruct((BLOCKS, len(LOWER), TILE, TILE), F32),
            jax.ShapeDtypeStruct((BLOCKS, 16, 8, TILE), F32),
        ),
        in_specs=[pl.BlockSpec(memory_space=pltpu.SMEM)] + full_specs(2),
        out_specs=(pl.BlockSpec(memory_space=VMEM),) * 3,
        scratch_shapes=[VMEM((BLOCKS, 4, 4, TILE, TILE), F32), VMEM((BLOCKS, 16, 8, TILE), F32)],
        compiler_params=pltpu.CompilerParams(vmem_limit_bytes=20 << 20),
        cost_estimate=pl.CostEstimate(flops=25_000_000_000, bytes_accessed=50_000_000, transcendentals=0),
        name="factor",
    )(core, own, other)


def solve_kernel(
    feat_ref, pivot_ref, last_ref, lower_ref, own_ref, other_ref, s0, s1, s2, s3, ft_ref, labels_ref, coef_ref, res_ref, steps
):
    core = lax.rem(feat_ref[0], 2)
    for d, share_ref in enumerate((s0, s1, s2, s3)):
        origin = lax.rem(feat_ref[1] + 4 - d, 4)
        steps[pl.ds(pl.multiple_of(origin * 384, 128), 384), :] = share_ref[...].reshape(384, TILE)
    fit = jnp.zeros((ROWS, TILE), F32)
    for b in range(BLOCKS):
        block = slice(b * BLK, (b + 1) * BLK)
        parts = []
        gradient = steps[block, :] * (CLS / SAMPLES)
        for i in range(4):
            total = gradient[i * TILE : (i + 1) * TILE]
            for a in range(b):
                tiles = []
                for j in range(4):
                    feat, slot = divmod(CROSS.index((b, a, i, j)), CROSS_SLOTS)
                    place = (slot % 4, feat // 2, slice(None), slice(8 * (slot // 4), 8 * (slot // 4) + 8))
                    tile = jnp.where(core == feat % 2, own_ref[place], other_ref[place])
                    tiles.append(tile.reshape(TILE, TILE))
                strip = jnp.concatenate(tiles, axis=1) * (1.0 / SAMPLES)
                total = total - dot_exact(strip, steps[a * BLK : (a + 1) * BLK, :])
            parts.append(total)
        forward = []
        for i in range(4):
            total = parts[i]
            if i:
                strip = jnp.concatenate([lower_ref[b, LOWER.index((i, j))] for j in range(i)], axis=1)
                total = total + dot_exact(strip, jnp.concatenate(parts[:i], axis=0))
            forward.append(dot_exact(pivot_ref[b, i] if i < 3 else last_ref[b], total))
        for i in range(4):
            total = forward[i]
            if i < 3:
                strip = jnp.concatenate([lower_ref[b, LOWER.index((j, i))] for j in range(i + 1, 4)], axis=0)
                total = total + dot_tn_exact(strip, jnp.concatenate(forward[i + 1 :], axis=0))
            steps[b * BLK + i * TILE : b * BLK + (i + 1) * TILE, :] = total
        value = steps[block, :]
        coef_ref[block, :] = value[:, :SHARE]
        high = value.astype(BF16)
        left = value - high.astype(F32)
        middle = left.astype(BF16)
        low = (left - middle.astype(F32)).astype(BF16)
        terms = lax.dot_general(
            ft_ref[block, :],
            jnp.concatenate([high, middle, low], axis=1),
            (((0,), (0,)), ((), ())),
            preferred_element_type=F32,
        )
        fit = fit + ((terms[:, 2 * TILE :] + terms[:, TILE : 2 * TILE]) + terms[:, :TILE])
    local = (labels_ref[...] - feat_ref[0] * SHARE).astype(F32)
    upright = jnp.broadcast_to(local, (TILE, ROWS)).T
    classes = lax.broadcasted_iota(jnp.int32, (ROWS, TILE), 1).astype(F32)
    targets = jnp.where(upright == classes, 1.0, 0.0)
    res_ref[...] = (targets - fit / CLS)[:, :SHARE]


def solve(feat, pivots, last, lower, own, other, shares, features, labels):
    return pl.pallas_call(
        solve_kernel,
        out_shape=(
            jax.ShapeDtypeStruct((BLOCKS * BLK, SHARE), F32),
            jax.ShapeDtypeStruct((ROWS, SHARE), F32),
        ),
        in_specs=[pl.BlockSpec(memory_space=pltpu.SMEM)] + full_specs(11),
        out_specs=(pl.BlockSpec(memory_space=VMEM), pl.BlockSpec(memory_space=VMEM)),
        scratch_shapes=[VMEM((BLOCKS * BLK, TILE), F32)],
        compiler_params=pltpu.CompilerParams(vmem_limit_bytes=24 << 20),
        name="solve",
    )(feat, pivots, last, lower, own, other, *shares, features, labels)


def gather_by_exchange(value, axis, size):
    copies = jnp.broadcast_to(value[None], (size,) + value.shape)
    return lax.all_to_all(copies, axis, 0, 0, tiled=True)


def swap_cores(value):
    return lax.ppermute(value, "c", [(0, 1), (1, 0)])


def per_device(images, labels, filters, biases):
    core = lax.axis_index("c")
    feat = (lax.axis_index("x") * 2 + core).reshape(1)
    core1 = core.reshape(1)
    panel = local_features(images, filters.reshape(LOCAL, 108), biases)
    own = lax.all_gather(panel, "x", axis=0)
    other = swap_cores(own)
    pair = jnp.where(core == 0, jnp.stack([own, other]), jnp.stack([other, own]))
    features = pair.reshape(2, 4, BLOCKS, 64, ROWS).transpose(2, 1, 0, 3, 4).reshape(BLOCKS * BLK, ROWS)

    pieces = local_products(feat, features, labels.reshape(1, ROWS))
    pieces = lax.all_to_all(pieces.reshape(4, 16 * 48, TILE), "y", 0, 0, tiled=True)
    pieces = jnp.sum(pieces, axis=0).reshape(16, 48, TILE)
    pieces = jnp.sum(lax.all_to_all(pieces, "z", 0, 0, tiled=True), axis=0)
    column = gather_by_exchange(pieces, "z", 16)

    share = column[:, 24:]
    steps = [share] + [lax.ppermute(share, "y", [(i, (i + d) % 4) for i in range(4)]) for d in (1, 2, 3)]
    diag_own = gather_by_exchange(column[:, :8], ("y", "x"), 16).reshape(DIAG_SLOTS, 4, TILE, TILE)
    diag_other = swap_cores(diag_own)
    crossing, diag_own = lax.optimization_barrier((column[:, 8:24], diag_own))
    cross_own = gather_by_exchange(crossing, ("y", "x"), 16)

    pivots, lower, last = factor(core1, diag_own, diag_other)
    last, cross_own, steps = lax.optimization_barrier((last, cross_own, steps))
    cross_own = cross_own.reshape(4, 4, 16, 16, TILE)
    cross_other = swap_cores(cross_own)
    last = last_pivots(last)
    return solve(jnp.stack([feat[0], lax.axis_index("y")]), pivots, last, lower, cross_own, cross_other, steps, features, labels.reshape(1, ROWS))


def solution(mesh):
    split = Mesh(mesh.devices.reshape(4, 16, 4, 2), ("y", "z", "x", "c"))
    samp, feat = ("y", "z"), ("x", "c")
    return jax.shard_map(
        per_device,
        mesh=split,
        in_specs=(P(samp, None), P(samp), P(None, feat, None), P(None, feat)),
        out_specs=(P(None, feat), P(samp, feat)),
        check_vma=False,
    )
```
